128 devices in a mesh: tier: 8 (over z, core), member: 16 (over y, x).
Axes of the slice: x: 4, y: 4, z: 4, core: 2. Of those that a mesh axis runs over, the one named last changes fastest.
Arguments:
- density: float32 [1024, 2, 9216], P(('tier', 'member')), may hold values from -6 to 6
- hamiltonian: float32 [96, 96], replicated, may hold values from -4 to 4, as said below
- coupling: float32 [96, 96, 96], replicated, may hold values from -2 to 2, as said below
- decay_rate: float32 [96], replicated, may hold values from 0.3 to 2
- corr_real: float32 [96], replicated, may hold values from 0.3 to 1.5
- corr_imag: float32 [96], replicated, may hold values from -1 to 1
- up_member: int32 [1024, 1], P(('tier', 'member')), may hold values from 0 to 15; in each aligned block of 8 rows (0 to 7, 8 to 15, ...) at most 2 rows name the same one
- up_slot: int32 [1024, 1], P(('tier', 'member')), may hold values from 0 to 7
- up_mode: int32 [1024, 1], P(('tier', 'member')), may hold values from 0 to 95
- down_member: int32 [1024, 1], P(('tier', 'member')), may hold values from 0 to 15; in each aligned block of 8 rows (0 to 7, 8 to 15, ...) at most 2 rows name the same one
- down_slot: int32 [1024, 1], P(('tier', 'member')), may hold values from 0 to 7
- down_mode: int32 [1024, 1], P(('tier', 'member')), may hold values from 0 to 95
Outputs:
- evolved: float32 [1024, 2, 9216], P(('tier', 'member'))
The draws below stay inside these ranges and needn't reach their ends.
Inputs may be any that keep to these rules, and one draw needn't show every extreme that they name: `up_member`: among the rows of one device no member index is named by more than 2 rows, a bound that some block reaches. `down_member`: among the rows of one device no member index is named by more than 2 rows, a bound that some block reaches. `hamiltonian`: Symmetric. `coupling`: each mode's matrix is symmetric.
All inputs are finite; a program needn't handle non-finite values.
Results may differ from the reference program's by a relative error of at most 0.0003.
Values sent between devices are 32-bit elements; how exact they have to be, the bound alone decides.
No kernel may reach another device: no remote copies, remote signals or barrier semaphores. Data moves between devices by JAX's collectives and lax.ppermute only.
A program may use at most 128 MiB of HBM per device.

```python
import math
import jax
import jax.numpy as jnp
import numpy as np
from jax import lax

NSYS = 96
NMODE = 96
LINKS = 1
M_DEV = 8
CAP = 2
TOTAL = 1024
N_TIER = 8
N_MEMBER = 16


def draw_hamiltonian(key, part):
    key = jax.random.fold_in(key, 11)
    key_base, key_site = jax.random.split(key)
    base = jnp.clip(jax.random.normal(key_base, (NSYS, NSYS), jnp.float32), -6.0, 6.0)
    symmetric = (base + base.T) / jnp.sqrt(2.0 * NSYS)
    site_energy = jax.random.uniform(key_site, (NSYS,), jnp.float32, -1.0, 1.0)
    return symmetric + jnp.diag(site_energy)


def draw_coupling(key, part):
    key = jax.random.fold_in(key, 23)
    base = jnp.clip(jax.random.normal(key, (NMODE, NSYS, NSYS), jnp.float32), -6.0, 6.0)
    return 0.5 * (base + jnp.swapaxes(base, 1, 2)) / jnp.sqrt(2.0 * NSYS)


def touch_ends(entries, rng, least, largest):
    longest = entries.shape.index(max(entries.shape))
    spots = []
    for shift in (0, 1):
        where = [jax.random.randint(jax.random.fold_in(rng, axis), (), 0, length) for axis, length in enumerate(entries.shape)]
        where[longest] = (where[longest] + shift) % entries.shape[longest]
        spots.append(tuple(where))
    return entries.at[spots[0]].set(least).at[spots[1]].set(largest)


def shard_levels(rng, dims, cuts, least, top_value):
    def one(dim, blocks):
        steps = jax.random.uniform(jax.random.fold_in(jax.random.fold_in(rng, 6), dim), (blocks,), jnp.float32, least / len(cuts), top_value / len(cuts))
        return jnp.repeat(jnp.exp(steps), dims[dim] // blocks).reshape((-1,) + (1,) * (len(dims) - dim - 1))

    level = one(*cuts[0])
    for cut in cuts[1:]:
        level = level * one(*cut)
    return level


def deal_out(rng, own, number, rows, number_of, top, bound, skew):
    sequence = jax.random.permutation(rng, number_of)
    crowded, ordinary = portions_of(number_of, rows * top, bound, skew, True), portions_of(number_of, rows * top, bound, skew, False)
    places = jnp.arange(number_of)

    def named(sizes, turn):
        used = int((sizes > 0).sum())
        fixed = max(1, used // 4)
        moved = fixed + (places - fixed + turn * (used - fixed)) % max(1, number_of - fixed)
        return jnp.zeros((number_of,), jnp.int32).at[sequence[jnp.where(places < fixed, places, moved)]].set(jnp.asarray(sizes, jnp.int32))

    sizes = jnp.where(number % 4 == 0, named(crowded, number // 4), named(ordinary, number - number // 4 - 1))
    mixed = jax.random.permutation(jax.random.fold_in(own, 3), number_of)
    source_of, taker = mixed[0:number_of // 2 * 2:2], mixed[1:number_of // 2 * 2:2]
    slack = jnp.minimum(sizes[source_of] - 1, bound - sizes[taker]) // 2
    slack = jnp.where((source_of == sequence[0]) | (taker == sequence[0]) | (sizes[taker] == 0), 0, jnp.maximum(slack, 0))
    moved = jax.random.randint(jax.random.fold_in(own, 4), (number_of // 2,), 0, 1 << 20) % (slack + 1)
    sizes = sizes.at[source_of].add(-moved).at[taker].add(moved)
    items = jnp.searchsorted(jnp.cumsum(sizes), jnp.arange(rows * top), side="right").astype(jnp.int32)
    table = items.reshape(top, rows).T
    table = table[jax.random.permutation(jax.random.fold_in(own, 1), rows)]
    turn = jax.random.randint(jax.random.fold_in(own, 2), (rows, 1), 0, top)
    return jnp.take_along_axis(table, (jnp.arange(top)[None, :] + turn) % top, axis=1)


def portions_of(number_of, total, bound, slope, full):
    loads = [(1 << 20) // math.isqrt(standing ** slope) + 1 for standing in range(1, number_of + 1)]
    largest = bound if full else min(bound, max(-(-total // number_of), total * loads[0] // sum(loads)))
    least = 1 if total - largest >= number_of - 1 else 0
    given, spare = [largest] + [least] * (number_of - 1), total - largest - least * (number_of - 1)
    while spare > 0:
        movable = [i for i in range(1, number_of) if given[i] < largest] or [i for i in range(1, number_of) if given[i] < bound]
        pool, budget = sum([loads[i] for i in movable]), spare
        for i in movable:
            addition = min(bound - given[i], max(1, budget * loads[i] // pool), spare)
            given[i] = given[i] + addition
            spare = spare - addition
    return np.array(given)


def bell_draw(stream_key, dims, width, most, cuts=(), kind=jnp.bfloat16):
    array = jax.random.normal(stream_key, dims, jnp.float32) * width
    if len(cuts) > 0:
        array = shard_levels(stream_key, dims, cuts, -0.22, 0.18) * array
    return jnp.clip(array, min=-most, max=most).astype(kind)


def setup_inputs(seed: int = 0) -> dict:
    arg_keys = jax.random.split(jax.random.key(seed), 13)
    density = bell_draw(arg_keys[0], (TOTAL, 2, NSYS * NSYS), 1.0, 6.0, ((0, 128),), jnp.float32)
    hamiltonian = draw_hamiltonian(jax.random.fold_in(arg_keys[12], 71), 0)
    coupling = draw_coupling(jax.random.fold_in(arg_keys[12], 71), 0)
    decay_rate = jnp.clip(jnp.exp(jax.random.uniform(arg_keys[3], (NMODE,), jnp.float32, math.log(0.3), math.log(2.0))), 0.3, 2.0)
    corr_real = jnp.clip(jnp.exp(jax.random.uniform(arg_keys[4], (NMODE,), jnp.float32, math.log(0.3), math.log(1.5))), 0.3, 1.5)
    corr_imag = jnp.clip(jax.random.uniform(arg_keys[5], (NMODE,), jnp.float32, -1.0, 1.0), -1.0, 1.0)
    up_member_keys = jax.random.split(jax.random.fold_in(arg_keys[6], 1), TOTAL // M_DEV)
    up_member_turns = jax.random.permutation(jax.random.fold_in(arg_keys[6], 3), TOTAL // M_DEV)
    up_member = jax.vmap(lambda own, number: deal_out(jax.random.fold_in(arg_keys[6], 2), own, number, M_DEV, N_MEMBER, 1, CAP, 2))(up_member_keys, up_member_turns).reshape((TOTAL, 1))
    up_slot = touch_ends(jax.random.randint(arg_keys[7], (TOTAL, LINKS), 0, M_DEV), jax.random.fold_in(arg_keys[7], 1), 0, M_DEV - 1).astype(jnp.int32)
    up_mode = touch_ends(jax.random.randint(arg_keys[8], (TOTAL, LINKS), 0, NMODE), jax.random.fold_in(arg_keys[8], 1), 0, NMODE - 1).astype(jnp.int32)
    down_member_keys = jax.random.split(jax.random.fold_in(arg_keys[9], 1), TOTAL // M_DEV)
    down_member_turns = jax.random.permutation(jax.random.fold_in(arg_keys[9], 3), TOTAL // M_DEV)
    down_member = jax.vmap(lambda own, number: deal_out(jax.random.fold_in(arg_keys[9], 2), own, number, M_DEV, N_MEMBER, 1, CAP, 2))(down_member_keys, down_member_turns).reshape((TOTAL, 1))
    down_slot = touch_ends(jax.random.randint(arg_keys[10], (TOTAL, LINKS), 0, M_DEV), jax.random.fold_in(arg_keys[10], 1), 0, M_DEV - 1).astype(jnp.int32)
    down_mode = touch_ends(jax.random.randint(arg_keys[11], (TOTAL, LINKS), 0, NMODE), jax.random.fold_in(arg_keys[11], 1), 0, NMODE - 1).astype(jnp.int32)
    return dict(density=density, hamiltonian=hamiltonian, coupling=coupling, decay_rate=decay_rate, corr_real=corr_real, corr_imag=corr_imag, up_member=up_member, up_slot=up_slot, up_mode=up_mode, down_member=down_member, down_slot=down_slot, down_mode=down_mode)


time_step = 0.08

def matprod(left, right):
    return jnp.einsum('...ik,...kj->...ij', left, right, precision=lax.Precision.HIGHEST)

def linksum(left, right):
    return jnp.einsum('slik,slkj->sij', left, right, precision=lax.Precision.HIGHEST)

def own_terms(hamiltonian, states):
    real_part = states[:, 0]
    imag_part = states[:, 1]
    first = matprod(hamiltonian, imag_part) - matprod(imag_part, hamiltonian)
    second = matprod(real_part, hamiltonian) - matprod(hamiltonian, real_part)
    return jnp.stack([first, second], axis=1)

def lift_terms(operators, values):
    real_part = values[:, :, 0]
    imag_part = values[:, :, 1]
    first = linksum(operators, imag_part) - linksum(imag_part, operators)
    second = linksum(real_part, operators) - linksum(operators, real_part)
    return jnp.stack([first, second], axis=1)

def lower_terms(operators, values, coef_real, coef_imag):
    real_part = values[:, :, 0]
    imag_part = values[:, :, 1]
    scale_re = coef_real[:, :, None, None]
    scale_im = coef_imag[:, :, None, None]
    left_re = scale_re * real_part - scale_im * imag_part
    left_im = scale_im * real_part + scale_re * imag_part
    right_re = scale_re * real_part + scale_im * imag_part
    right_im = scale_im * real_part - scale_re * imag_part
    cross_real = linksum(operators, left_re) - linksum(right_re, operators)
    cross_imag = linksum(operators, left_im) + linksum(right_im, operators)
    return jnp.stack([cross_imag, -cross_real], axis=1)

def runge_kutta(states, derivative):
    section_one = derivative(states)
    section_two = derivative(states + 0.5 * time_step * section_one)
    section_three = derivative(states + 0.5 * time_step * section_two)
    section_four = derivative(states + time_step * section_three)
    return states + time_step / 6.0 * (section_one + 2.0 * section_two + 2.0 * section_three + section_four)

def reference(density, hamiltonian, coupling, decay_rate, corr_real, corr_imag, up_member, up_slot, up_mode, down_member, down_slot, down_mode):
    row_block = M_DEV * N_MEMBER
    block_count = N_TIER * N_MEMBER
    states = density.reshape(TOTAL, 2, NSYS, NSYS)
    tier_of = jnp.arange(TOTAL, dtype=jnp.int32) // row_block
    up_base = (tier_of + 1) * row_block + up_member[:, 0] * M_DEV
    up_index = jnp.clip(up_base[:, None] + up_slot, 0, TOTAL - 1).astype(jnp.int32)
    up_valid = (tier_of + 1 < N_TIER).astype(jnp.float32)
    down_base = (tier_of - 1) * row_block + down_member[:, 0] * M_DEV
    down_index = jnp.clip(down_base[:, None] + down_slot, 0, TOTAL - 1).astype(jnp.int32)
    tier_float = tier_of.astype(jnp.float32)
    up_weight = jnp.sqrt(tier_float + 1.0) * up_valid
    down_weight = jnp.sqrt(tier_float)
    damping = tier_float / LINKS * lax.optimization_barrier(jnp.sum(decay_rate[down_mode], axis=1))
    coef_real = corr_real[down_mode]
    coef_imag = corr_imag[down_mode]

    def derivative(current):

        def one_block(block_no):
            start_row = (block_no * M_DEV).astype(jnp.int32)
            up_rows = lax.dynamic_slice_in_dim(up_index, start_row, M_DEV)
            down_rows = lax.dynamic_slice_in_dim(down_index, start_row, M_DEV)
            up_ops = coupling[lax.dynamic_slice_in_dim(up_mode, start_row, M_DEV)]
            down_ops = coupling[lax.dynamic_slice_in_dim(down_mode, start_row, M_DEV)]
            local_states = lax.dynamic_slice_in_dim(current, start_row, M_DEV)
            lifted = lift_terms(up_ops, current[up_rows])
            lowered = lower_terms(down_ops, current[down_rows], lax.dynamic_slice_in_dim(coef_real, start_row, M_DEV), lax.dynamic_slice_in_dim(coef_imag, start_row, M_DEV))
            weight_up = lax.dynamic_slice_in_dim(up_weight, start_row, M_DEV)[:, None, None, None]
            weight_down = lax.dynamic_slice_in_dim(down_weight, start_row, M_DEV)[:, None, None, None]
            local_damp = lax.dynamic_slice_in_dim(damping, start_row, M_DEV)[:, None, None, None]
            return own_terms(hamiltonian, local_states) + weight_up * lifted + weight_down * lowered - local_damp * local_states
        pieces = lax.map(one_block, jnp.arange(block_count, dtype=jnp.int32))
        return pieces.reshape(TOTAL, 2, NSYS, NSYS)
    evolved = runge_kutta(states, derivative)
    return evolved.reshape(TOTAL, 2, NSYS * NSYS)
```

```python
import functools

import jax
import jax.numpy as jnp
from jax import lax
from jax.experimental import pallas as pl
from jax.experimental.pallas import tpu as pltpu
from jax.sharding import PartitionSpec as P

STEP = 0.08
N = 96
M = 8
ROWS = 144
HALF = 72
TIERS = 8
SIDE = 4
F32 = jnp.float32
BF16 = jnp.bfloat16
CHUNK = 128
SEND_A, SEND_B, OWN_A, OWN_B, UP_MODE, DOWN_MODE, COUNT = 0, 32, 64, 80, 96, 120, 144


def ring(axis_shift, value):
    rows = value.shape[0] // 2
    back = lax.ppermute(value, "member", axis_shift(1))
    front = lax.ppermute(value, "member", axis_shift(-1))
    first = lax.ppermute(back[:rows], "member", axis_shift(1))
    second = lax.ppermute(front[rows:], "member", axis_shift(-1))
    return jnp.concatenate([value, back, front, first, second], axis=0)


def along_x(step):
    return [(y * SIDE + x, y * SIDE + (x + step) % SIDE) for y in range(SIDE) for x in range(SIDE)]


def along_y(step):
    return [(y * SIDE + x, (y + step) % SIDE * SIDE + x) for y in range(SIDE) for x in range(SIDE)]


def gathered(state):
    first = ring(along_y, ring(along_x, state[:, :HALF]))
    second = ring(along_x, ring(along_y, state[:, HALF:]))
    return first, second


def passed_along(value, steps):
    low, high = max(0, -steps), min(TIERS, TIERS - steps)
    return lax.ppermute(value, "tier", [(source, source + steps) for source in range(low, high)])


def index_kernel(table, place, corr_real, corr_imag, decay, index, scale):
    tier, member_y, member_x = place[0], place[1], place[2]
    member = member_y * SIDE + member_x

    def entry(block, field, slot):
        return table[block * (6 * M) + field * M + slot]

    def block_of(level, who):
        return jnp.clip(level, 0, TIERS - 1) * (SIDE * SIDE) + who

    def spot(distance):
        return jnp.where(distance == 0, 0, jnp.where(distance == 3, 1, jnp.where(distance == 1, 2, 3)))

    def places(who, slot):
        at_y = spot(jnp.bitwise_and(who // SIDE - member_y + SIDE, SIDE - 1))
        at_x = spot(jnp.bitwise_and(jnp.bitwise_and(who, SIDE - 1) - member_x + SIDE, SIDE - 1))
        return (at_y * SIDE + at_x) * M + slot, (at_x * SIDE + at_y) * M + slot

    def put(base_a, base_b, at, pair):
        index[base_a + at] = pair[0]
        index[base_b + at] = pair[1]

    def node(level, block, slot, at, rate):
        mode = entry(block, 5, slot)
        index[UP_MODE + at] = entry(block, 2, slot)
        index[DOWN_MODE + at] = mode
        scale[at] = corr_real[mode]
        scale[3 * M + at] = corr_imag[mode]
        scale[6 * M + at] = rate * decay[mode]

    own, above, below = block_of(tier, member), block_of(tier + 1, member), block_of(tier - 1, member)
    above2, below2 = block_of(tier + 2, member), block_of(tier - 2, member)
    level = tier.astype(F32)

    def one(m, carry):
        up = block_of(tier + 1, entry(own, 0, m))
        up_slot = entry(own, 1, m)
        down = block_of(tier - 1, entry(own, 3, m))
        down_slot = entry(own, 4, m)
        node(tier, own, m, m, STEP * level)
        node(tier + 1, up, up_slot, M + m, STEP * (level + 1.0))
        node(tier - 1, down, down_slot, 2 * M + m, STEP * jnp.maximum(level - 1.0, 0.0))
        put(OWN_A, OWN_B, m, places(entry(up, 3, up_slot), entry(up, 4, up_slot)))
        put(OWN_A, OWN_B, M + m, places(entry(down, 0, down_slot), entry(down, 1, down_slot)))
        put(SEND_A, SEND_B, m, places(entry(below, 0, m), entry(below, 1, m)))
        put(SEND_A, SEND_B, M + m, places(entry(above, 3, m), entry(above, 4, m)))
        middle = block_of(tier - 1, entry(below2, 0, m))
        slot = entry(below2, 1, m)
        put(SEND_A, SEND_B, 2 * M + m, places(entry(middle, 0, slot), entry(middle, 1, slot)))
        middle = block_of(tier + 1, entry(above2, 3, m))
        slot = entry(above2, 4, m)
        put(SEND_A, SEND_B, 3 * M + m, places(entry(middle, 3, slot), entry(middle, 4, slot)))
        return carry

    lax.fori_loop(0, M, one, 0)


def make_index(table, place, corr_real, corr_imag, decay):
    smem = pl.BlockSpec(memory_space=pltpu.SMEM)
    return pl.pallas_call(
        index_kernel,
        in_specs=[smem] * 5,
        out_specs=[smem, smem],
        out_shape=[jax.ShapeDtypeStruct((COUNT,), jnp.int32), jax.ShapeDtypeStruct((9 * M,), F32)],
        name="links",
    )(table, place, corr_real, corr_imag, decay)


def split(value):
    high = value.astype(BF16)
    return high, (value - high.astype(F32)).astype(BF16)


def operator_kernel(index, weight, hamiltonian, up_op, down_op, left, right):
    kind = pl.program_id(0) // M
    left[...] = jnp.zeros_like(left)
    right[...] = jnp.zeros_like(right)
    parts = (STEP * hamiltonian[...], weight[kind] * up_op[0], weight[3 + kind] * down_op[0])
    for place, part in enumerate(parts):
        high, low = split(part)
        for turn, piece in enumerate((high, low, high)):
            left[0, :, (3 * place + turn) * CHUNK : (3 * place + turn) * CHUNK + N] = piece
        for turn, piece in enumerate((high, high, low)):
            right[0, (3 * place + turn) * CHUNK : (3 * place + turn) * CHUNK + N, 0:N] = piece


def make_operators(index, weight, hamiltonian, coupling):
    return pl.pallas_call(
        operator_kernel,
        grid_spec=pltpu.PrefetchScalarGridSpec(
            num_scalar_prefetch=2,
            grid=(3 * M,),
            in_specs=[
                pl.BlockSpec((N, N), lambda n, index, weight: (0, 0)),
                pl.BlockSpec((1, N, N), lambda n, index, weight: (index[UP_MODE + n], 0, 0)),
                pl.BlockSpec((1, N, N), lambda n, index, weight: (index[DOWN_MODE + n], 0, 0)),
            ],
            out_specs=[
                pl.BlockSpec((1, N, 9 * CHUNK), lambda n, index, weight: (n, 0, 0)),
                pl.BlockSpec((1, 9 * CHUNK, CHUNK), lambda n, index, weight: (n, 0, 0)),
            ],
        ),
        out_shape=[
            jax.ShapeDtypeStruct((3 * M, N, 9 * CHUNK), BF16),
            jax.ShapeDtypeStruct((3 * M, 9 * CHUNK, CHUNK), BF16),
        ],
        name="operators",
    )(index, weight, hamiltonian, coupling, coupling)


def pick_kernel(index, first, second, *refs):
    outs, done = refs[:4], refs[4]
    copies = []
    for kind, out in enumerate(outs):
        for m in range(M):
            at = kind * M + m
            copies.append(pltpu.make_async_copy(first.at[index[SEND_A + at]], out.at[m, pl.ds(0, HALF)], done.at[2 * at]))
            copies.append(pltpu.make_async_copy(second.at[index[SEND_B + at]], out.at[m, pl.ds(HALF, HALF)], done.at[2 * at + 1]))
    for copy in copies:
        copy.start()
    for copy in copies:
        copy.wait()


def picked(index, first, second):
    anywhere = pl.BlockSpec(memory_space=pl.ANY)
    return pl.pallas_call(
        pick_kernel,
        in_specs=[pl.BlockSpec(memory_space=pltpu.SMEM), anywhere, anywhere],
        out_specs=[anywhere] * 4,
        out_shape=[jax.ShapeDtypeStruct((M, ROWS, 128), F32)] * 4,
        scratch_shapes=[pltpu.SemaphoreType.DMA((8 * M,))],
        name="pick",
    )(index, first, second)


def unpack(source, target):
    lane = lax.broadcasted_iota(jnp.int32, (24, 128), 1)
    for part in range(2):
        a, b, c = (source[pl.ds(2 * k + part, 24, stride=6), :] for k in range(3))
        target[pl.ds(part * N, 24, stride=4), :] = a
        target[pl.ds(part * N + 1, 24, stride=4), :] = jnp.where(lane < 32, pltpu.roll(a, 32, 1), pltpu.roll(b, 32, 1))
        target[pl.ds(part * N + 2, 24, stride=4), :] = jnp.where(lane < 64, pltpu.roll(b, 64, 1), pltpu.roll(c, 64, 1))
        target[pl.ds(part * N + 3, 24, stride=4), :] = pltpu.roll(c, 96, 1)


def pack(source, target):
    lane = lax.broadcasted_iota(jnp.int32, (24, 128), 1)
    for part in range(2):
        a, b, c, d = (source[pl.ds(part * N + k, 24, stride=4), :] for k in range(4))
        b, c, d = pltpu.roll(b, 96, 1), pltpu.roll(c, 64, 1), pltpu.roll(d, 32, 1)
        target[pl.ds(part, 24, stride=6), :] = jnp.where(lane < 96, a, b)
        target[pl.ds(part + 2, 24, stride=6), :] = jnp.where(lane < 64, b, c)
        target[pl.ds(part + 4, 24, stride=6), :] = jnp.where(lane < 32, c, d)


def applied(own, up, down, left, right, cr, ci, damp):
    def halves(value):
        return value[:N], value[N:]

    xr, xi = halves(own)
    ur, ui = halves(up)
    dr, di = halves(down)
    rr, ri, ir, ii = cr * dr, cr * di, ci * dr, ci * di
    lefts, rights = [], []
    for (ar, ai), (br, bi) in (((xr, xi), (xr, xi)), ((ur, ui), (ur, ui)), ((rr - ii, ir + ri), (rr + ii, ri - ir))):
        high, low = split(jnp.concatenate([ar, ai], axis=1))
        lefts += [high, high, low]
        high, low = split(jnp.concatenate([br, bi], axis=0))
        rights += [high, low, high]
    pad = jnp.zeros((CHUNK - N, 2 * CHUNK), BF16)
    tall = jnp.concatenate([piece for value in lefts for piece in (value, pad)], axis=0)
    wide = jnp.concatenate(rights, axis=1)
    from_left = jnp.dot(left, tall, preferred_element_type=F32)
    from_right = jnp.dot(wide, right, preferred_element_type=F32)
    real = from_left[:, CHUNK:] - from_right[N:] - damp * xr
    imag = from_right[:N] - from_left[:, :CHUNK] - damp * xi
    return jnp.concatenate([real, imag], axis=0)


def stage_kernel(last, index, scale, *refs):
    own, up, down, up2, down2, ud_a, ud_b, du_a, du_b, left, right = refs[:11]
    if last:
        before, result, raw, plain, level1, level2 = refs[11:]
    else:
        result, total, raw, plain, level1, level2 = refs[11:]
    m = pl.program_id(0)
    for place, source in enumerate((own, up, down, up2, down2)):
        unpack(source.at[0], plain.at[place])
    for place, (a, b) in enumerate(((ud_a, ud_b), (du_a, du_b))):
        raw[place, 0:HALF, :] = a[0]
        raw[place, HALF:ROWS, :] = b[0]
        unpack(raw.at[place], plain.at[5 + place])
    for kind, (x, u, d) in enumerate(((0, 1, 2), (1, 3, 5), (2, 6, 4))):
        at = kind * M + m
        level1[kind] = applied(
            plain[x], plain[u], plain[d], left[kind, 0], right[kind, 0], scale[at], scale[3 * M + at], scale[6 * M + at]
        )
    second = applied(
        level1[0], level1[1], level1[2], left[0, 0], right[0, 0], scale[m], scale[3 * M + m], scale[6 * M + m]
    )
    if last:
        level2[...] = before[0] + (1.0 / 6.0) * level1[0] + (1.0 / 24.0) * second
        pack(level2, result.at[0])
    else:
        level2[...] = second
        pack(level2, result.at[0])
        total[0] = plain[0] + level1[0] + 0.5 * second


def stage(index, scale, own, received, first, second, left, right, before):
    last = before is not None
    whole = pl.BlockSpec((1, ROWS, 128), lambda m, index, scale: (m, 0, 0))
    plain = pl.BlockSpec((1, 2 * N, 128), lambda m, index, scale: (m, 0, 0))

    def chosen(base):
        return pl.BlockSpec((1, HALF, 128), lambda m, index, scale: (index[base + m], 0, 0))

    result = jax.ShapeDtypeStruct((M, ROWS, 128), F32)
    sums = jax.ShapeDtypeStruct((M, 2 * N, 128), F32)
    return pl.pallas_call(
        functools.partial(stage_kernel, last),
        grid_spec=pltpu.PrefetchScalarGridSpec(
            num_scalar_prefetch=2,
            grid=(M,),
            in_specs=[whole] * 5
            + [chosen(OWN_A), chosen(OWN_B), chosen(OWN_A + M), chosen(OWN_B + M)]
            + [
                pl.BlockSpec((3, 1, N, 9 * CHUNK), lambda m, index, scale: (0, m, 0, 0)),
                pl.BlockSpec((3, 1, 9 * CHUNK, CHUNK), lambda m, index, scale: (0, m, 0, 0)),
            ]
            + ([plain] if last else []),
            out_specs=[whole] if last else [whole, plain],
            scratch_shapes=[
                pltpu.VMEM((2, ROWS, 128), F32),
                pltpu.VMEM((7, 2 * N, 128), F32),
                pltpu.VMEM((3, 2 * N, 128), F32),
                pltpu.VMEM((2 * N, 128), F32),
            ],
        ),
        out_shape=[result] if last else [result, sums],
        compiler_params=pltpu.CompilerParams(vmem_limit_bytes=48 * 1024 * 1024),
        name="stage",
    )(index, scale, own, *received, first, second, first, second, left, right, *([before] if last else []))


def shards(
    density,
    hamiltonian,
    coupling,
    decay_rate,
    corr_real,
    corr_imag,
    up_member,
    up_slot,
    up_mode,
    down_member,
    down_slot,
    down_mode,
):
    tier, member = lax.axis_index("tier"), lax.axis_index("member")
    fields = jnp.stack([f[:, 0] for f in (up_member, up_slot, up_mode, down_member, down_slot, down_mode)])
    table = lax.all_gather(fields.reshape(-1), ("tier", "member"), tiled=True)
    place = jnp.stack([tier, member // SIDE, member % SIDE]).astype(jnp.int32)
    levels = jnp.stack([tier, tier + 1, tier - 1]).astype(F32)
    ups = jnp.where(levels + 1.0 < TIERS, jnp.sqrt(levels + 1.0), 0.0)
    downs = jnp.sqrt(jnp.maximum(levels, 0.0))
    weight = STEP * jnp.concatenate([ups, downs])
    index, scale = make_index(table, place, corr_real, corr_imag, decay_rate)
    left, right = make_operators(index, weight, hamiltonian, coupling)
    left, right = left.reshape(3, M, N, 9 * CHUNK), right.reshape(3, M, 9 * CHUNK, CHUNK)

    def exchange(state):
        first, second = gathered(state)
        sent = picked(index, first, second)
        return [passed_along(value, steps) for value, steps in zip(sent, (-1, 1, -2, 2))], first, second

    state = density.reshape(M, 2, HALF, 128).transpose(0, 2, 1, 3).reshape(M, ROWS, 128)
    received, first, second = exchange(state)
    state2, total = stage(index, scale, state, received, first, second, left, right, None)
    received, first, second = exchange(state2)
    (result,) = stage(index, scale, state2, received, first, second, left, right, total)
    return result.reshape(M, HALF, 2, 128).transpose(0, 2, 1, 3).reshape(M, 2, N * N)


def solution(mesh):
    return jax.shard_map(
        shards,
        mesh=mesh,
        in_specs=(P(("tier", "member"), None, None),) + (P(),) * 5 + (P(("tier", "member"), None),) * 6,
        out_specs=P(("tier", "member"), None, None),
        check_vma=False,
    )
```

```python
import functools

import jax
import jax.numpy as jnp
from jax import lax
from jax.experimental import pallas as pl
from jax.experimental.pallas import tpu as pltpu
from jax.sharding import PartitionSpec as P

STEP = 0.08
N = 96
M = 8
ROWS = 144
PIECE = 9
MEMBERS = 16
TIERS = 8
WEIGHT = 9 * M
FIELDS = 6 * M
F32 = jnp.float32
BF16 = jnp.bfloat16
CHUNK = 128


def passed_along(value, steps):
    low, high = max(0, -steps), min(TIERS, TIERS - steps)
    return lax.ppermute(value, "tier", [(source, source + steps) for source in range(low, high)])


def entry(table, level, member, field, slot):
    return table[(level * MEMBERS + member) * FIELDS + field * M + slot]


def nodes_kernel(table, place, corr_real, corr_imag, decay, weight, mode, scale):
    tier, member = place[0], place[1]
    level = tier.astype(F32)

    def node(at, where, rate):
        down_mode = entry(table, *where[:2], 5, where[2])
        mode[at] = entry(table, *where[:2], 2, where[2])
        mode[3 * M + at] = down_mode
        scale[at] = corr_real[down_mode]
        scale[3 * M + at] = corr_imag[down_mode]
        scale[6 * M + at] = rate * decay[down_mode]

    def one(m, carry):
        node(m, (0, member, m), STEP * level)
        node(M + m, (1, entry(table, 0, member, 0, m), entry(table, 0, member, 1, m)), STEP * (level + 1.0))
        node(
            2 * M + m,
            (2, entry(table, 0, member, 3, m), entry(table, 0, member, 4, m)),
            STEP * jnp.maximum(level - 1.0, 0.0),
        )
        return carry

    lax.fori_loop(0, M, one, 0)
    for kind in range(6):
        scale[WEIGHT + kind] = weight[kind]


def make_nodes(table, place, corr_real, corr_imag, decay, weight):
    smem = pl.BlockSpec(memory_space=pltpu.SMEM)
    return pl.pallas_call(
        nodes_kernel,
        in_specs=[smem] * 6,
        out_specs=[smem, smem],
        out_shape=[jax.ShapeDtypeStruct((6 * M,), jnp.int32), jax.ShapeDtypeStruct((WEIGHT + 6,), F32)],
        name="nodes",
    )(table, place, corr_real, corr_imag, decay, weight)


def split(value):
    high = value.astype(BF16)
    return high, (value - high.astype(F32)).astype(BF16)


def deal_kernel(state, links, out):
    for member in range(MEMBERS):
        for m in range(M):
            out[member, m * PIECE : (m + 1) * PIECE, :] = state[m, member * PIECE : (member + 1) * PIECE, :]
        out[member, M * PIECE :, :] = links[...]


def dealt(state, links):
    return pl.pallas_call(
        deal_kernel,
        out_shape=jax.ShapeDtypeStruct((MEMBERS, M * PIECE + 8, 128), F32),
        compiler_params=pltpu.CompilerParams(vmem_limit_bytes=16 * 1024 * 1024),
        name="deal",
    )(state, links)


def pick_near_kernel(table, own, out):
    def one(member, carry):
        for m in range(M):
            for kind, first in ((0, 0), (1, 3)):
                who, slot = entry(table, 0, member, first, m), entry(table, 0, member, first + 1, m)
                who, slot = (entry(table, kind + 1, who, 3 - first + field, slot) for field in range(2))
                row = (kind * M + m) * PIECE
                out[member, row : row + PIECE, :] = own[who, pl.ds(slot * PIECE, PIECE), :]
        return carry

    lax.fori_loop(0, MEMBERS, one, 0)


def pick_other_kernel(table, place, mate, cross, above2, below2, out):
    def one(above, below, member, carry):
        for m in range(M):
            for kind, source, source2, first in ((0, above, above2, 0), (1, below, below2, 3)):
                who, slot = entry(table, 0, member, first, m), entry(table, 0, member, first + 1, m)
                row = (m * 4 + kind) * PIECE
                out[member, row : row + PIECE, :] = source[who, pl.ds(slot * PIECE, PIECE), :]
                who, slot = (entry(table, kind + 1, who, first + field, slot) for field in range(2))
                row += 2 * PIECE
                out[member, row : row + PIECE, :] = source2[who, pl.ds(slot * PIECE, PIECE), :]
        return carry

    lower_core = jnp.bitwise_and(place[0], 1) == 0
    pl.when(lower_core)(lambda: lax.fori_loop(0, MEMBERS, functools.partial(one, mate, cross), None))
    pl.when(jnp.logical_not(lower_core))(lambda: lax.fori_loop(0, MEMBERS, functools.partial(one, cross, mate), None))


def picked(kernel, kinds, scalars, blocks):
    return pl.pallas_call(
        kernel,
        in_specs=[pl.BlockSpec(memory_space=pltpu.SMEM)] * len(scalars)
        + [pl.BlockSpec(memory_space=pltpu.VMEM)] * len(blocks),
        out_specs=pl.BlockSpec(memory_space=pltpu.VMEM),
        out_shape=jax.ShapeDtypeStruct((MEMBERS, kinds * M * PIECE, 128), F32),
        compiler_params=pltpu.CompilerParams(vmem_limit_bytes=16 * 1024 * 1024),
        name="pick",
    )(*scalars, *blocks)


def unpack(source, target):
    lane = lax.broadcasted_iota(jnp.int32, (24, 128), 1)
    for part in range(2):
        a, b, c = (source[pl.ds(2 * k + part, 24, stride=6), :] for k in range(3))
        target[pl.ds(part * N, 24, stride=4), :] = a
        target[pl.ds(part * N + 1, 24, stride=4), :] = jnp.where(lane < 32, pltpu.roll(a, 32, 1), pltpu.roll(b, 32, 1))
        target[pl.ds(part * N + 2, 24, stride=4), :] = jnp.where(lane < 64, pltpu.roll(b, 64, 1), pltpu.roll(c, 64, 1))
        target[pl.ds(part * N + 3, 24, stride=4), :] = pltpu.roll(c, 96, 1)


def pack(source, target):
    lane = lax.broadcasted_iota(jnp.int32, (24, 128), 1)
    for part in range(2):
        a, b, c, d = (source[pl.ds(part * N + k, 24, stride=4), :] for k in range(4))
        b, c, d = pltpu.roll(b, 96, 1), pltpu.roll(c, 64, 1), pltpu.roll(d, 32, 1)
        target[pl.ds(part, 24, stride=6), :] = jnp.where(lane < 96, a, b)
        target[pl.ds(part + 2, 24, stride=6), :] = jnp.where(lane < 64, b, c)
        target[pl.ds(part + 4, 24, stride=6), :] = jnp.where(lane < 32, c, d)


def halved(value):
    high, low = split(value)
    return (high[:N], high[N:]), (low[:N], low[N:])


def commuted(*terms):
    lefts, rights, tall, wide = [], [], [], []
    pad = jnp.zeros((CHUNK - N, 2 * CHUNK), BF16)
    thin = pad[:, :CHUNK]
    for operator, a, b in terms:
        high, low = split(operator)
        lefts += [high, low, high]
        rights += [high, thin, high, thin, low, thin]
        high, low = (jnp.concatenate(piece, axis=1) for piece in a)
        tall += [high, pad, high, pad, low, pad]
        high, low = (jnp.concatenate(piece, axis=0) for piece in b)
        wide += [high, low, high]
    from_left = jnp.dot(
        jnp.concatenate(lefts, axis=1), jnp.concatenate(tall, axis=0), preferred_element_type=F32
    )
    from_right = jnp.dot(
        jnp.concatenate(wide, axis=1), jnp.concatenate(rights, axis=0), preferred_element_type=F32
    )
    return jnp.concatenate([from_left[:, CHUNK:] - from_right[N:], from_right[:N] - from_left[:, :CHUNK]], axis=0)


def widened(operator):
    return jnp.concatenate([operator, jnp.zeros((N, CHUNK - N), F32)], axis=1)


def plainly(operator, value):
    pieces = halved(value)
    return operator, pieces, pieces


def with_factor(operator, value, cr, ci):
    dr, di = value[:N], value[N:]
    rr, ri, ir, ii = cr * dr, cr * di, ci * dr, ci * di
    a, b = jnp.concatenate([rr - ii, ir + ri], axis=0), jnp.concatenate([rr + ii, ri - ir], axis=0)
    return operator, halved(a), halved(b)


def assembled(source, row, raw, target):
    for member in range(MEMBERS):
        raw[member * PIECE : (member + 1) * PIECE, :] = source[member, pl.ds(row, PIECE), :]
    unpack(raw, target)


def factor(scale, kind, m):
    return scale[kind * M + m], scale[3 * M + kind * M + m]


def early_kernel(last, mode, scale, state, near, core, *refs):
    ops, refs = refs[: 2 * TOGETHER], refs[2 * TOGETHER :]
    first, first_up, first_down, raw, plain = refs[-5:]
    for turn in range(TOGETHER):
        m = pl.program_id(0) * TOGETHER + turn
        above_op, below_op = ops[2 * turn : 2 * turn + 2]
        if last:
            own = state[turn]
        else:
            unpack(state.at[turn], refs[0].at[turn])
            own = refs[0][turn]
        for kind in range(2):
            assembled(near, (kind * M + m) * PIECE, raw.at[turn, kind], plain.at[turn, kind])
        first[turn] = commuted(plainly(widened(STEP * core[...]), own)) - scale[6 * M + m] * own
        first_up[turn] = commuted(
            with_factor(widened(scale[WEIGHT + 4] * above_op[0]), plain[turn, 0], *factor(scale, 1, m))
        )
        first_down[turn] = commuted(plainly(widened(scale[WEIGHT + 2] * below_op[0]), plain[turn, 1]))


def late_kernel(last, mode, scale, other, core, *refs):
    ops, (base, part, part_up, part_down), refs = refs[: 4 * TOGETHER], refs[4 * TOGETHER :][:4], refs[4 * TOGETHER + 4 :]
    if last:
        result, raw, plain = refs
    else:
        result, following, total, raw, plain = refs
    for turn in range(TOGETHER):
        m = pl.program_id(0) * TOGETHER + turn
        up_op, down_op, above_op, below_op = ops[4 * turn : 4 * turn + 4]
        for kind in range(4):
            assembled(other, (turn * 4 + kind) * PIECE, raw.at[turn, kind], plain.at[turn, kind])
        up, down, up2, down2 = (plain[turn, kind] for kind in range(4))
        hamiltonian = widened(STEP * core[...])
        up_op, down_op = widened(scale[WEIGHT] * up_op[0]), widened(scale[WEIGHT + 3] * down_op[0])
        own_factor = factor(scale, 0, m)
        up_pieces = halved(up)
        first = part[turn] + commuted((up_op, up_pieces, up_pieces), with_factor(down_op, down, *own_factor))
        first_up = (
            part_up[turn]
            + commuted((hamiltonian, up_pieces, up_pieces), plainly(widened(scale[WEIGHT + 1] * above_op[0]), up2))
            - scale[7 * M + m] * up
        )
        first_down = (
            part_down[turn]
            + commuted(
                plainly(hamiltonian, down),
                with_factor(widened(scale[WEIGHT + 5] * below_op[0]), down2, *factor(scale, 2, m)),
            )
            - scale[8 * M + m] * down
        )
        second = (
            commuted(plainly(hamiltonian, first), plainly(up_op, first_up), with_factor(down_op, first_down, *own_factor))
            - scale[6 * M + m] * first
        )
        if last:
            plain[turn, 0] = base[turn] + (1.0 / 6.0) * first + (1.0 / 24.0) * second
            pack(plain.at[turn, 0], result.at[turn])
        else:
            following[turn] = second
            plain[turn, 0] = second
            total[turn] = base[turn] + first + 0.5 * second
            pack(plain.at[turn, 0], raw.at[turn, 0])
            for member in range(MEMBERS):
                result[member, pl.ds(m * PIECE, PIECE), :] = raw[turn, 0, member * PIECE : (member + 1) * PIECE, :]


TOGETHER = 2
PLAIN = pl.BlockSpec((TOGETHER, 2 * N, 128), lambda step, mode, scale: (step, 0, 0))
WHOLE = pl.BlockSpec((TOGETHER, ROWS, 128), lambda step, mode, scale: (step, 0, 0))
SUMS = pltpu.HBM((M, 2 * N, 128), F32)


def all_of(shape):
    return pl.BlockSpec(shape, lambda step, mode, scale: (0,) * len(shape))


def operator_specs(*lists):
    return [
        pl.BlockSpec((1, N, N), lambda step, mode, scale, at=at * M + turn: (mode[step * TOGETHER + at], 0, 0))
        for turn in range(TOGETHER)
        for at in lists
    ]


def by_matrix(kernel, name, in_specs, out_specs, out_shape, raws, plains):
    return pl.pallas_call(
        kernel,
        grid_spec=pltpu.PrefetchScalarGridSpec(
            num_scalar_prefetch=2,
            grid=(M // TOGETHER,),
            in_specs=in_specs,
            out_specs=out_specs,
            scratch_shapes=[pltpu.VMEM((TOGETHER, raws, ROWS, 128), F32), pltpu.VMEM((TOGETHER, plains, 2 * N, 128), F32)],
        ),
        out_shape=out_shape,
        compiler_params=pltpu.CompilerParams(vmem_limit_bytes=32 * 1024 * 1024),
        name=name,
    )


def kept(*values):
    return [pltpu.with_memory_space_constraint(value, pltpu.HBM) for value in values]


def early(nodes, state, near, operators, last):
    hamiltonian, coupling = operators
    specs = [PLAIN if last else WHOLE, all_of(near.shape), all_of(hamiltonian.shape)] + operator_specs(4, 2)
    outs = 3 if last else 4
    call = by_matrix(functools.partial(early_kernel, last), "early", specs, [PLAIN] * outs, [SUMS] * outs, 2, 2)
    return call(*nodes, *kept(state), near, hamiltonian, *kept(*[coupling] * (2 * TOGETHER)))


def late(nodes, other, operators, base, parts, last):
    hamiltonian, coupling = operators
    specs = [pl.BlockSpec((MEMBERS, TOGETHER * 4 * PIECE, 128), lambda step, mode, scale: (0, step, 0))]
    specs += [all_of(hamiltonian.shape)] + operator_specs(0, 3, 1, 5) + [PLAIN] * 4
    if last:
        outs = [WHOLE], [jax.ShapeDtypeStruct((M, ROWS, 128), F32)]
    else:
        blocks = (MEMBERS, M * PIECE, 128)
        outs = [all_of(blocks), PLAIN, PLAIN], [jax.ShapeDtypeStruct(blocks, F32), SUMS, SUMS]
    call = by_matrix(functools.partial(late_kernel, last), "late", specs, *outs, 4, 4)
    return call(*nodes, other, hamiltonian, *kept(*[coupling] * (4 * TOGETHER), base, *parts))


def shards(
    density,
    hamiltonian,
    coupling,
    decay_rate,
    corr_real,
    corr_imag,
    up_member,
    up_slot,
    up_mode,
    down_member,
    down_slot,
    down_mode,
):
    tier, member = lax.axis_index("tier"), lax.axis_index("member")
    fields = jnp.stack([f[:, 0] for f in (up_member, up_slot, up_mode, down_member, down_slot, down_mode)])
    fields = fields.reshape(1, FIELDS).astype(F32)
    links = jnp.pad(fields, ((0, 7), (0, 128 - FIELDS)))
    place = jnp.stack([tier, member]).astype(jnp.int32)
    levels = jnp.stack([tier, tier + 1, tier - 1]).astype(F32)
    ups = jnp.where(levels + 1.0 < TIERS, jnp.sqrt(levels + 1.0), 0.0)
    downs = jnp.sqrt(jnp.maximum(levels, 0.0))
    weight = STEP * jnp.concatenate([ups, downs])

    def swapped(blocks):
        return lax.all_to_all(blocks, "member", split_axis=0, concat_axis=0, tiled=True)

    def link_fields(tier_blocks):
        return tier_blocks[:, M * PIECE, :FIELDS].reshape(-1).astype(jnp.int32)

    def two_steps(own, table, state, operators, nodes, before):
        last = before is not None
        mate = lax.ppermute(own, "tier", [(source, source ^ 1) for source in range(TIERS)])
        above2, below2 = passed_along(own, -2), passed_along(own, 2)
        near = swapped(picked(pick_near_kernel, 2, [table], [own]))
        cross = jnp.where(tier % 2 == 0, above2, below2)
        cross = lax.ppermute(cross, "tier", [(source, source ^ 1) for source in range(TIERS)])
        other = swapped(picked(pick_other_kernel, 4, [table, place], [mate, cross, above2, below2]))
        *base, part, part_up, part_down = early(nodes, state, near, operators, last)
        return late(nodes, other, operators, before if last else base[0], (part, part_up, part_down), last)

    state = density.reshape(M, 2, ROWS // 2, 128).transpose(0, 2, 1, 3).reshape(M, ROWS, 128)
    own = swapped(dealt(state, links))
    table = link_fields(own)
    table = jnp.concatenate([table, passed_along(table, -1), passed_along(table, 1)])
    own, table = lax.optimization_barrier((own, table))
    nodes = make_nodes(table, place, corr_real, corr_imag, decay_rate, weight)
    operators = hamiltonian, coupling
    blocks, state, total = two_steps(own, table, state, operators, nodes, None)
    (result,) = two_steps(swapped(blocks), table, state, operators, nodes, total)
    return result.reshape(M, ROWS // 2, 2, 128).transpose(0, 2, 1, 3).reshape(M, 2, N * N)


def solution(mesh):
    return jax.shard_map(
        shards,
        mesh=mesh,
        in_specs=(P(("tier", "member"), None, None),) + (P(),) * 5 + (P(("tier", "member"), None),) * 6,
        out_specs=P(("tier", "member"), None, None),
        check_vma=False,
    )
```

```python
import functools

import jax
import jax.numpy as jnp
from jax import lax
from jax.experimental import pallas as pl
from jax.experimental.pallas import tpu as pltpu
from jax.sharding import PartitionSpec as P

STEP = 0.08
N = 96
M = 8
ROWS = 144
PIECE = 9
MEMBERS = 16
TIERS = 8
WEIGHT = 9 * M
FIELDS = 6 * M
F32 = jnp.float32
BF16 = jnp.bfloat16
CHUNK = 128


def passed_along(value, steps):
    low, high = max(0, -steps), min(TIERS, TIERS - steps)
    return lax.ppermute(value, "tier", [(source, source + steps) for source in range(low, high)])


def entry(table, level, member, field, slot):
    return table[(level * MEMBERS + member) * FIELDS + field * M + slot]


def nodes_kernel(table, place, corr_real, corr_imag, decay, weight, mode, scale):
    tier, member = place[0], place[1]
    level = tier.astype(F32)

    def node(at, where, rate):
        down_mode = entry(table, *where[:2], 5, where[2])
        mode[at] = entry(table, *where[:2], 2, where[2])
        mode[3 * M + at] = down_mode
        scale[at] = corr_real[down_mode]
        scale[3 * M + at] = corr_imag[down_mode]
        scale[6 * M + at] = rate * decay[down_mode]

    def one(m, carry):
        node(m, (0, member, m), STEP * level)
        node(M + m, (1, entry(table, 0, member, 0, m), entry(table, 0, member, 1, m)), STEP * (level + 1.0))
        node(
            2 * M + m,
            (2, entry(table, 0, member, 3, m), entry(table, 0, member, 4, m)),
            STEP * jnp.maximum(level - 1.0, 0.0),
        )
        return carry

    lax.fori_loop(0, M, one, 0)
    for kind in range(6):
        scale[WEIGHT + kind] = weight[kind]


def make_nodes(table, place, corr_real, corr_imag, decay, weight):
    smem = pl.BlockSpec(memory_space=pltpu.SMEM)
    return pl.pallas_call(
        nodes_kernel,
        in_specs=[smem] * 6,
        out_specs=[smem, smem],
        out_shape=[jax.ShapeDtypeStruct((6 * M,), jnp.int32), jax.ShapeDtypeStruct((WEIGHT + 6,), F32)],
        name="nodes",
    )(table, place, corr_real, corr_imag, decay, weight)


def split(value):
    high = value.astype(BF16)
    return high, (value - high.astype(F32)).astype(BF16)


def deal_kernel(state, links, out):
    for member in range(MEMBERS):
        for m in range(M):
            out[member, m * PIECE : (m + 1) * PIECE, :] = state[m, member * PIECE : (member + 1) * PIECE, :]
        out[member, M * PIECE :, :] = links[...]


def dealt(state, links):
    return pl.pallas_call(
        deal_kernel,
        out_shape=jax.ShapeDtypeStruct((MEMBERS, M * PIECE + 8, 128), F32),
        compiler_params=pltpu.CompilerParams(vmem_limit_bytes=16 * 1024 * 1024),
        name="deal",
    )(state, links)


def pick_near_kernel(table, own, out):
    def one(member, carry):
        for m in range(M):
            for kind, first in ((0, 0), (1, 3)):
                who, slot = entry(table, 0, member, first, m), entry(table, 0, member, first + 1, m)
                who, slot = (entry(table, kind + 1, who, 3 - first + field, slot) for field in range(2))
                row = (kind * M + m) * PIECE
                out[member, row : row + PIECE, :] = own[who, pl.ds(slot * PIECE, PIECE), :]
        return carry

    lax.fori_loop(0, MEMBERS, one, 0)


def pick_other_kernel(table, place, mate, cross, above2, below2, out):
    def one(above, below, member, carry):
        for m in range(M):
            for kind, source, source2, first in ((0, above, above2, 0), (1, below, below2, 3)):
                who, slot = entry(table, 0, member, first, m), entry(table, 0, member, first + 1, m)
                row = (m * 4 + kind) * PIECE
                out[member, row : row + PIECE, :] = source[who, pl.ds(slot * PIECE, PIECE), :]
                who, slot = (entry(table, kind + 1, who, first + field, slot) for field in range(2))
                row += 2 * PIECE
                out[member, row : row + PIECE, :] = source2[who, pl.ds(slot * PIECE, PIECE), :]
        return carry

    lower_core = jnp.bitwise_and(place[0], 1) == 0
    pl.when(lower_core)(lambda: lax.fori_loop(0, MEMBERS, functools.partial(one, mate, cross), None))
    pl.when(jnp.logical_not(lower_core))(lambda: lax.fori_loop(0, MEMBERS, functools.partial(one, cross, mate), None))


def picked(kernel, kinds, scalars, blocks):
    return pl.pallas_call(
        kernel,
        in_specs=[pl.BlockSpec(memory_space=pltpu.SMEM)] * len(scalars)
        + [pl.BlockSpec(memory_space=pltpu.VMEM)] * len(blocks),
        out_specs=pl.BlockSpec(memory_space=pltpu.VMEM),
        out_shape=pltpu.HBM((MEMBERS, kinds * M * PIECE, 128), F32),
        compiler_params=pltpu.CompilerParams(vmem_limit_bytes=16 * 1024 * 1024),
        name="pick",
    )(*scalars, *blocks)


def unpack(source, target):
    lane = lax.broadcasted_iota(jnp.int32, (24, 128), 1)
    for part in range(2):
        a, b, c = (source[pl.ds(2 * k + part, 24, stride=6), :] for k in range(3))
        target[pl.ds(part * N, 24, stride=4), :] = a
        target[pl.ds(part * N + 1, 24, stride=4), :] = jnp.where(lane < 32, pltpu.roll(a, 32, 1), pltpu.roll(b, 32, 1))
        target[pl.ds(part * N + 2, 24, stride=4), :] = jnp.where(lane < 64, pltpu.roll(b, 64, 1), pltpu.roll(c, 64, 1))
        target[pl.ds(part * N + 3, 24, stride=4), :] = pltpu.roll(c, 96, 1)


def pack(source, target):
    lane = lax.broadcasted_iota(jnp.int32, (24, 128), 1)
    for part in range(2):
        a, b, c, d = (source[pl.ds(part * N + k, 24, stride=4), :] for k in range(4))
        b, c, d = pltpu.roll(b, 96, 1), pltpu.roll(c, 64, 1), pltpu.roll(d, 32, 1)
        target[pl.ds(part, 24, stride=6), :] = jnp.where(lane < 96, a, b)
        target[pl.ds(part + 2, 24, stride=6), :] = jnp.where(lane < 64, b, c)
        target[pl.ds(part + 4, 24, stride=6), :] = jnp.where(lane < 32, c, d)


def halved(value):
    high, low = split(value)
    return (high[:N], high[N:]), (low[:N], low[N:])


def commuted(*terms):
    lefts, tall, wide_high, wide_low, both, highs = [], [], [], [], [], []
    pad = jnp.zeros((CHUNK - N, 2 * CHUNK), BF16)
    for operator, a, b in terms:
        high, low = split(operator)
        lefts += [high, low, high]
        both += [jnp.concatenate([high, low], axis=1), pad]
        highs += [high, pad[:, :CHUNK]]
        high, low = (jnp.concatenate(piece, axis=1) for piece in a)
        tall += [high, pad, high, pad, low, pad]
        high, low = (jnp.concatenate(piece, axis=0) for piece in b)
        wide_high.append(high)
        wide_low.append(low)

    def product(left, right):
        return jnp.dot(jnp.concatenate(left, axis=1), jnp.concatenate(right, axis=0), preferred_element_type=F32)

    from_left = product(lefts, tall)
    from_right = product(wide_high, both)
    from_right = from_right[:, :CHUNK] + from_right[:, CHUNK:] + product(wide_low, highs)
    return jnp.concatenate([from_left[:, CHUNK:] - from_right[N:], from_right[:N] - from_left[:, :CHUNK]], axis=0)


def widened(operator):
    return jnp.concatenate([operator, jnp.zeros((N, CHUNK - N), F32)], axis=1)


def plainly(operator, value):
    pieces = halved(value)
    return operator, pieces, pieces


def with_factor(operator, value, cr, ci):
    dr, di = value[:N], value[N:]
    rr, ri, ir, ii = cr * dr, cr * di, ci * dr, ci * di
    a, b = jnp.concatenate([rr - ii, ir + ri], axis=0), jnp.concatenate([rr + ii, ri - ir], axis=0)
    return operator, halved(a), halved(b)


def assembled(source, row, raw, target):
    for member in range(MEMBERS):
        raw[member * PIECE : (member + 1) * PIECE, :] = source[member, pl.ds(row, PIECE), :]
    unpack(raw, target)


def factor(scale, kind, m):
    return scale[kind * M + m], scale[3 * M + kind * M + m]


def early_kernel(last, mode, scale, state, near, core, *refs):
    ops, refs = refs[: 4 * TOGETHER], refs[4 * TOGETHER :]
    part, total, raw, plain = refs[-4:]
    hamiltonian = widened(STEP * core[...])
    for turn in range(TOGETHER):
        m = pl.program_id(0) * TOGETHER + turn
        up_op, down_op, above_op, below_op = ops[4 * turn : 4 * turn + 4]
        if last:
            assembled(state, m * PIECE, raw.at[turn, 0], plain.at[turn, 0])
        else:
            unpack(state.at[turn], plain.at[turn, 0])
        for kind in range(2):
            assembled(near, (kind * M + m) * PIECE, raw.at[turn, 1 + kind], plain.at[turn, 1 + kind])
        own, up_down, down_up = (plain[turn, place] for place in range(3))
        first = commuted(plainly(hamiltonian, own)) - scale[6 * M + m] * own
        first_up = commuted(with_factor(widened(scale[WEIGHT + 4] * above_op[0]), up_down, *factor(scale, 1, m)))
        first_down = commuted(plainly(widened(scale[WEIGHT + 2] * below_op[0]), down_up))
        part[turn] = second_of(scale, m, hamiltonian, up_op, down_op, first, first_up, first_down)
        if last:
            before, before_first = refs[:2]
            total[turn] = before[turn] + before_first[turn] + 0.5 * own + (1.0 / 6.0) * first
        else:
            total[turn] = own + first


def second_of(scale, m, hamiltonian, up_op, down_op, first, first_up, first_down):
    up_op, down_op = widened(scale[WEIGHT] * up_op[0]), widened(scale[WEIGHT + 3] * down_op[0])
    return (
        commuted(
            plainly(hamiltonian, first), plainly(up_op, first_up), with_factor(down_op, first_down, *factor(scale, 0, m))
        )
        - scale[6 * M + m] * first
    )


def late_kernel(last, mode, scale, other, core, *refs):
    ops, part, refs = refs[: 4 * TOGETHER], refs[4 * TOGETHER], refs[4 * TOGETHER + 1 :]
    if last:
        total, result, raw, plain = refs
    else:
        result, kept_first, raw, plain = refs
    hamiltonian = widened(STEP * core[...])
    for turn in range(TOGETHER):
        m = pl.program_id(0) * TOGETHER + turn
        up_op, down_op, above_op, below_op = ops[4 * turn : 4 * turn + 4]
        for kind in range(4):
            assembled(other, (turn * 4 + kind) * PIECE, raw.at[turn, kind], plain.at[turn, kind])
        up, down, up2, down2 = (plain[turn, kind] for kind in range(4))
        up_pieces = halved(up)
        first = commuted(
            (widened(scale[WEIGHT] * up_op[0]), up_pieces, up_pieces),
            with_factor(widened(scale[WEIGHT + 3] * down_op[0]), down, *factor(scale, 0, m)),
        )
        first_up = (
            commuted((hamiltonian, up_pieces, up_pieces), plainly(widened(scale[WEIGHT + 1] * above_op[0]), up2))
            - scale[7 * M + m] * up
        )
        first_down = (
            commuted(
                plainly(hamiltonian, down),
                with_factor(widened(scale[WEIGHT + 5] * below_op[0]), down2, *factor(scale, 2, m)),
            )
            - scale[8 * M + m] * down
        )
        second = part[turn] + second_of(scale, m, hamiltonian, up_op, down_op, first, first_up, first_down)
        if last:
            plain[turn, 0] = total[turn] + (1.0 / 6.0) * first + (1.0 / 24.0) * second
            pack(plain.at[turn, 0], result.at[turn])
        else:
            kept_first[turn] = first
            plain[turn, 0] = second
            pack(plain.at[turn, 0], raw.at[turn, 0])
            for member in range(MEMBERS):
                result[member, pl.ds(m * PIECE, PIECE), :] = raw[turn, 0, member * PIECE : (member + 1) * PIECE, :]


TOGETHER = 2
PLAIN = pl.BlockSpec((TOGETHER, 2 * N, 128), lambda step, mode, scale: (step, 0, 0))
WHOLE = pl.BlockSpec((TOGETHER, ROWS, 128), lambda step, mode, scale: (step, 0, 0))
SUMS = pltpu.HBM((M, 2 * N, 128), F32)


def all_of(shape):
    return pl.BlockSpec(shape, lambda step, mode, scale: (0,) * len(shape))


def operator_specs(*lists):
    return [
        pl.BlockSpec((1, N, N), lambda step, mode, scale, at=at * M + turn: (mode[step * TOGETHER + at], 0, 0))
        for turn in range(TOGETHER)
        for at in lists
    ]


def by_matrix(kernel, name, in_specs, out_specs, out_shape, raws, plains):
    return pl.pallas_call(
        kernel,
        grid_spec=pltpu.PrefetchScalarGridSpec(
            num_scalar_prefetch=2,
            grid=(M // TOGETHER,),
            in_specs=in_specs,
            out_specs=out_specs,
            scratch_shapes=[pltpu.VMEM((TOGETHER, raws, ROWS, 128), F32), pltpu.VMEM((TOGETHER, plains, 2 * N, 128), F32)],
        ),
        out_shape=out_shape,
        compiler_params=pltpu.CompilerParams(vmem_limit_bytes=32 * 1024 * 1024),
        name=name,
    )


def kept(*values):
    return [pltpu.with_memory_space_constraint(value, pltpu.HBM) for value in values]


def early(nodes, state, near, operators, sums):
    hamiltonian, coupling = operators
    last = len(sums) > 0
    specs = [all_of(state.shape) if last else WHOLE, all_of(near.shape), all_of(hamiltonian.shape)]
    specs += operator_specs(0, 3, 4, 2) + [PLAIN] * len(sums)
    call = by_matrix(functools.partial(early_kernel, last), "early", specs, [PLAIN] * 2, [SUMS] * 2, 3, 3)
    return call(*nodes, state, near, *kept(hamiltonian, *[coupling] * (4 * TOGETHER), *sums))


def late(nodes, other, operators, part, total):
    hamiltonian, coupling = operators
    last = total is not None
    specs = [pl.BlockSpec((MEMBERS, TOGETHER * 4 * PIECE, 128), lambda step, mode, scale: (0, step, 0))]
    specs += [all_of(hamiltonian.shape)] + operator_specs(0, 3, 1, 5) + [PLAIN] * (1 + last)
    if last:
        outs = [WHOLE], [jax.ShapeDtypeStruct((M, ROWS, 128), F32)]
    else:
        blocks = (MEMBERS, M * PIECE, 128)
        outs = [all_of(blocks), PLAIN], [pltpu.HBM(blocks, F32), SUMS]
    call = by_matrix(functools.partial(late_kernel, last), "late", specs, *outs, 4, 4)
    return call(*nodes, other, *kept(hamiltonian, *[coupling] * (4 * TOGETHER), part, *[total] * last))


def shards(
    density,
    hamiltonian,
    coupling,
    decay_rate,
    corr_real,
    corr_imag,
    up_member,
    up_slot,
    up_mode,
    down_member,
    down_slot,
    down_mode,
):
    tier, member = lax.axis_index("tier"), lax.axis_index("member")
    fields = jnp.stack([f[:, 0] for f in (up_member, up_slot, up_mode, down_member, down_slot, down_mode)])
    fields = fields.reshape(1, FIELDS).astype(F32)
    links = jnp.pad(fields, ((0, 7), (0, 128 - FIELDS)))
    place = jnp.stack([tier, member]).astype(jnp.int32)
    levels = jnp.stack([tier, tier + 1, tier - 1]).astype(F32)
    ups = jnp.where(levels + 1.0 < TIERS, jnp.sqrt(levels + 1.0), 0.0)
    downs = jnp.sqrt(jnp.maximum(levels, 0.0))
    weight = STEP * jnp.concatenate([ups, downs])

    def swapped(blocks):
        return lax.all_to_all(blocks, "member", split_axis=0, concat_axis=0, tiled=True)

    def link_fields(tier_blocks):
        return tier_blocks[:, M * PIECE, :FIELDS].reshape(-1).astype(jnp.int32)

    def two_steps(own, table, state, operators, nodes, sums):
        mate = lax.ppermute(own, "tier", [(source, source ^ 1) for source in range(TIERS)])
        above2, below2 = passed_along(own, -2), passed_along(own, 2)
        near = swapped(picked(pick_near_kernel, 2, [table], [own]))
        cross = jnp.where(tier % 2 == 0, above2, below2)
        cross = lax.ppermute(cross, "tier", [(source, source ^ 1) for source in range(TIERS)])
        other = swapped(picked(pick_other_kernel, 4, [table, place], [mate, cross, above2, below2]))
        part, total = early(nodes, state, near, operators, sums)
        return total, late(nodes, other, operators, part, total if sums else None)

    state = density.reshape(M, 2, ROWS // 2, 128).transpose(0, 2, 1, 3).reshape(M, ROWS, 128)
    own = swapped(dealt(state, links))
    table = link_fields(own)
    table = jnp.concatenate([table, passed_along(table, -1), passed_along(table, 1)])
    own, table = lax.optimization_barrier((own, table))
    nodes = make_nodes(table, place, corr_real, corr_imag, decay_rate, weight)
    operators = hamiltonian, coupling
    start, (blocks, first) = two_steps(own, table, state, operators, nodes, ())
    _, (result,) = two_steps(swapped(blocks), table, blocks, operators, nodes, (start, first))
    return result.reshape(M, ROWS // 2, 2, 128).transpose(0, 2, 1, 3).reshape(M, 2, N * N)


def solution(mesh):
    return jax.shard_map(
        shards,
        mesh=mesh,
        in_specs=(P(("tier", "member"), None, None),) + (P(),) * 5 + (P(("tier", "member"), None),) * 6,
        out_specs=P(("tier", "member"), None, None),
        check_vma=False,
    )
```

```python
import functools

import jax
import jax.numpy as jnp
from jax import lax
from jax.experimental import pallas as pl
from jax.experimental.pallas import tpu as pltpu
from jax.sharding import PartitionSpec as P

STEP = 0.08
N = 96
M = 8
ROWS = 144
PIECE = 9
MEMBERS = 16
TIERS = 8
WEIGHT = 9 * M
FIELDS = 6 * M
F32 = jnp.float32
BF16 = jnp.bfloat16
CHUNK = 128


def passed_along(value, steps):
    low, high = max(0, -steps), min(TIERS, TIERS - steps)
    return lax.ppermute(value, "tier", [(source, source + steps) for source in range(low, high)])


def entry(table, level, member, field, slot):
    return table[(level * MEMBERS + member) * FIELDS + field * M + slot]


def nodes_kernel(table, place, corr_real, corr_imag, decay, weight, mode, scale, lists):
    tier, member = place[0], place[1]
    level = tier.astype(F32)

    def node(at, where, rate):
        down_mode = entry(table, *where[:2], 5, where[2])
        mode[at] = entry(table, *where[:2], 2, where[2])
        mode[3 * M + at] = down_mode
        scale[at] = corr_real[down_mode]
        scale[3 * M + at] = corr_imag[down_mode]
        scale[6 * M + at] = rate * decay[down_mode]

    def one(m, carry):
        node(m, (0, member, m), STEP * level)
        node(M + m, (1, entry(table, 0, member, 0, m), entry(table, 0, member, 1, m)), STEP * (level + 1.0))
        node(
            2 * M + m,
            (2, entry(table, 0, member, 3, m), entry(table, 0, member, 4, m)),
            STEP * jnp.maximum(level - 1.0, 0.0),
        )
        return carry

    lax.fori_loop(0, M, one, 0)
    for kind in range(6):
        scale[WEIGHT + kind] = weight[kind]

    def note(member, carry):
        for m in range(M):
            for kind in range(2):
                for far in range(3):
                    who, slot = chased(table, member, m, kind, far)
                    lists[(member * M + m) * 6 + kind * 3 + far] = who * M + slot
        return carry

    lax.fori_loop(0, MEMBERS, note, 0)


def make_nodes(table, place, corr_real, corr_imag, decay, weight):
    smem = pl.BlockSpec(memory_space=pltpu.SMEM)
    return pl.pallas_call(
        nodes_kernel,
        in_specs=[smem] * 6,
        out_specs=[smem] * 3,
        out_shape=[
            jax.ShapeDtypeStruct((6 * M,), jnp.int32),
            jax.ShapeDtypeStruct((WEIGHT + 6,), F32),
            jax.ShapeDtypeStruct((MEMBERS * M * 6,), jnp.int32),
        ],
        name="nodes",
    )(table, place, corr_real, corr_imag, decay, weight)


def split(value):
    high = value.astype(BF16)
    return high, (value - high.astype(F32)).astype(BF16)


def deal_kernel(state, links, out):
    for member in range(MEMBERS):
        for m in range(M):
            out[member, m * PIECE : (m + 1) * PIECE, :] = state[m, member * PIECE : (member + 1) * PIECE, :]
        out[member, M * PIECE :, :] = links[...]


def dealt(state, links):
    return pl.pallas_call(
        deal_kernel,
        out_shape=jax.ShapeDtypeStruct((MEMBERS, M * PIECE + 8, 128), F32),
        compiler_params=pltpu.CompilerParams(vmem_limit_bytes=16 * 1024 * 1024),
        name="deal",
    )(state, links)


def chased(table, member, m, kind, far):
    first = 3 * kind
    who, slot = entry(table, 0, member, first, m), entry(table, 0, member, first + 1, m)
    if far:
        then = first if far == 1 else 3 - first
        who, slot = (entry(table, kind + 1, who, then + field, slot) for field in range(2))
    return who, slot


def listed(lists, member, m, kind, far):
    place = lists[(member * M + m) * 6 + kind * 3 + far]
    return lax.shift_right_logical(place, 3), jnp.bitwise_and(place, M - 1)


def sent_out(held, out, done, member):
    return pltpu.make_async_copy(held.at[member], out.at[member], done.at[member])


def pick_near_kernel(find, links, own, out, held, done):
    def one(member, carry):
        for m in range(M):
            for kind in range(2):
                who, slot = find(links, member, m, kind, 2)
                row = (kind * M + m) * PIECE
                held[member, row : row + PIECE, :] = own[who, pl.ds(slot * PIECE, PIECE), :]
        sent_out(held, out, done, member).start()
        return carry

    lax.fori_loop(0, MEMBERS, one, 0)
    for member in range(MEMBERS):
        sent_out(held, out, done, member).wait()


def pick_other_kernel(find, links, place, mate, cross, above2, below2, out, held, done):
    def one(above, below, member, carry):
        for m in range(M):
            for kind, source, source2 in ((0, above, above2), (1, below, below2)):
                who, slot = find(links, member, m, kind, 0)
                row = (m * 4 + kind) * PIECE
                held[member, row : row + PIECE, :] = source[who, pl.ds(slot * PIECE, PIECE), :]
                who, slot = find(links, member, m, kind, 1)
                row += 2 * PIECE
                held[member, row : row + PIECE, :] = source2[who, pl.ds(slot * PIECE, PIECE), :]
        sent_out(held, out, done, member).start()
        return carry

    lower_core = jnp.bitwise_and(place[0], 1) == 0
    pl.when(lower_core)(lambda: lax.fori_loop(0, MEMBERS, functools.partial(one, mate, cross), None))
    pl.when(jnp.logical_not(lower_core))(lambda: lax.fori_loop(0, MEMBERS, functools.partial(one, cross, mate), None))
    for member in range(MEMBERS):
        sent_out(held, out, done, member).wait()


def picked(kernel, kinds, scalars, blocks):
    shape = (MEMBERS, kinds * M * PIECE, 128)
    return pl.pallas_call(
        kernel,
        in_specs=[pl.BlockSpec(memory_space=pltpu.SMEM)] * len(scalars)
        + [pl.BlockSpec(memory_space=pltpu.VMEM)] * len(blocks),
        out_specs=pl.BlockSpec(memory_space=pl.ANY),
        out_shape=pltpu.HBM(shape, F32),
        scratch_shapes=[pltpu.VMEM(shape, F32), pltpu.SemaphoreType.DMA((MEMBERS,))],
        compiler_params=pltpu.CompilerParams(vmem_limit_bytes=16 * 1024 * 1024),
        name="pick",
    )(*scalars, *blocks)


def unpack(source, target):
    lane = lax.broadcasted_iota(jnp.int32, (24, 128), 1)
    for part in range(2):
        a, b, c = (source[pl.ds(2 * k + part, 24, stride=6), :] for k in range(3))
        target[pl.ds(part * N, 24, stride=4), :] = a
        target[pl.ds(part * N + 1, 24, stride=4), :] = jnp.where(lane < 32, pltpu.roll(a, 32, 1), pltpu.roll(b, 32, 1))
        target[pl.ds(part * N + 2, 24, stride=4), :] = jnp.where(lane < 64, pltpu.roll(b, 64, 1), pltpu.roll(c, 64, 1))
        target[pl.ds(part * N + 3, 24, stride=4), :] = pltpu.roll(c, 96, 1)


def pack(source, target):
    lane = lax.broadcasted_iota(jnp.int32, (24, 128), 1)
    for part in range(2):
        a, b, c, d = (source[pl.ds(part * N + k, 24, stride=4), :] for k in range(4))
        b, c, d = pltpu.roll(b, 96, 1), pltpu.roll(c, 64, 1), pltpu.roll(d, 32, 1)
        target[pl.ds(part, 24, stride=6), :] = jnp.where(lane < 96, a, b)
        target[pl.ds(part + 2, 24, stride=6), :] = jnp.where(lane < 64, b, c)
        target[pl.ds(part + 4, 24, stride=6), :] = jnp.where(lane < 32, c, d)


def halved(value):
    high, low = split(value)
    return (high[:N], high[N:]), (low[:N], low[N:])


def commuted(*terms):
    lefts, tall, wide_high, wide_low, both, highs = [], [], [], [], [], []
    pad = jnp.zeros((CHUNK - N, 2 * CHUNK), BF16)
    for operator, a, b in terms:
        high, low = operator[0], operator[1]
        lefts += [high, low, high]
        both += [jnp.concatenate([high, low], axis=1), pad]
        highs += [high, pad[:, :CHUNK]]
        high, low = (jnp.concatenate(piece, axis=1) for piece in a)
        tall += [high, pad, high, pad, low, pad]
        high, low = (jnp.concatenate(piece, axis=0) for piece in b)
        wide_high.append(high)
        wide_low.append(low)

    def product(left, right):
        return jnp.dot(jnp.concatenate(left, axis=1), jnp.concatenate(right, axis=0), preferred_element_type=F32)

    from_left = product(lefts, tall)
    from_right = product(wide_high, both)
    from_right = from_right[:, :CHUNK] + from_right[:, CHUNK:] + product(wide_low, highs)
    return jnp.concatenate([from_left[:, CHUNK:] - from_right[N:], from_right[:N] - from_left[:, :CHUNK]], axis=0)


def plainly(operator, value):
    pieces = halved(value)
    return operator, pieces, pieces


def with_factor(operator, value, cr, ci):
    dr, di = value[:N], value[N:]
    rr, ri, ir, ii = cr * dr, cr * di, ci * dr, ci * di
    a, b = jnp.concatenate([rr - ii, ir + ri], axis=0), jnp.concatenate([rr + ii, ri - ir], axis=0)
    return operator, halved(a), halved(b)


def assembled(source, row, raw, target):
    for member in range(MEMBERS):
        raw[member * PIECE : (member + 1) * PIECE, :] = source[member, pl.ds(row, PIECE), :]
    unpack(raw, target)


def operators_kernel(mode, scale, hamiltonian, coupling, out, held, done):
    copies = [pltpu.make_async_copy(coupling.at[mode[at]], held.at[at], done.at[at]) for at in range(6 * M)]
    for copy in copies:
        copy.start()

    def keep(at, operator):
        operator = jnp.concatenate([operator, jnp.zeros((N, CHUNK - N), F32)], axis=1)
        out[at, 0], out[at, 1] = split(operator)

    keep(6 * M, STEP * hamiltonian[...])
    for at, copy in enumerate(copies):
        copy.wait()
        keep(at, scale[WEIGHT + at // M] * held[at])


def make_operators(mode, scale, hamiltonian, coupling):
    smem, vmem = pl.BlockSpec(memory_space=pltpu.SMEM), pl.BlockSpec(memory_space=pltpu.VMEM)
    return pl.pallas_call(
        operators_kernel,
        in_specs=[smem, smem, vmem, pl.BlockSpec(memory_space=pl.ANY)],
        out_specs=vmem,
        out_shape=pltpu.HBM((6 * M + 1, 2, N, CHUNK), BF16),
        scratch_shapes=[pltpu.VMEM((6 * M, N, N), F32), pltpu.SemaphoreType.DMA((6 * M,))],
        compiler_params=pltpu.CompilerParams(vmem_limit_bytes=16 * 1024 * 1024),
        name="operators",
    )(mode, scale, hamiltonian, coupling)


def factor(scale, kind, m):
    return scale[kind * M + m], scale[3 * M + kind * M + m]


def early_kernel(last, scale, state, near, core, *refs):
    ops, refs = refs[: 4 * TOGETHER], refs[4 * TOGETHER :]
    part, total, raw, plain = refs[-4:]
    hamiltonian = core[0]
    for turn in range(TOGETHER):
        m = pl.program_id(0) * TOGETHER + turn
        up_op, down_op, above_op, below_op = ops[4 * turn : 4 * turn + 4]
        if last:
            assembled(state, m * PIECE, raw.at[turn, 0], plain.at[turn, 0])
        else:
            unpack(state.at[turn], plain.at[turn, 0])
        for kind in range(2):
            assembled(near, (kind * M + m) * PIECE, raw.at[turn, 1 + kind], plain.at[turn, 1 + kind])
        own, up_down, down_up = (plain[turn, place] for place in range(3))
        first = commuted(plainly(hamiltonian, own)) - scale[6 * M + m] * own
        first_up = commuted(with_factor(above_op[0], up_down, *factor(scale, 1, m)))
        first_down = commuted(plainly(below_op[0], down_up))
        part[turn] = second_of(scale, m, hamiltonian, up_op, down_op, first, first_up, first_down)
        if last:
            before, before_first = refs[:2]
            total[turn] = before[turn] + before_first[turn] + 0.5 * own + (1.0 / 6.0) * first
        else:
            total[turn] = own + first


def second_of(scale, m, hamiltonian, up_op, down_op, first, first_up, first_down):
    return (
        commuted(
            plainly(hamiltonian, first),
            plainly(up_op[0], first_up),
            with_factor(down_op[0], first_down, *factor(scale, 0, m)),
        )
        - scale[6 * M + m] * first
    )


def late_kernel(last, scale, other, core, *refs):
    ops, part, refs = refs[: 4 * TOGETHER], refs[4 * TOGETHER], refs[4 * TOGETHER + 1 :]
    if last:
        total, result, raw, plain = refs
    else:
        result, kept_first, raw, plain = refs
    hamiltonian = core[0]
    for turn in range(TOGETHER):
        m = pl.program_id(0) * TOGETHER + turn
        up_op, down_op, above_op, below_op = ops[4 * turn : 4 * turn + 4]
        for kind in range(4):
            assembled(other, (turn * 4 + kind) * PIECE, raw.at[turn, kind], plain.at[turn, kind])
        up, down, up2, down2 = (plain[turn, kind] for kind in range(4))
        up_pieces = halved(up)
        first = commuted(
            (up_op[0], up_pieces, up_pieces),
            with_factor(down_op[0], down, *factor(scale, 0, m)),
        )
        first_up = (
            commuted((hamiltonian, up_pieces, up_pieces), plainly(above_op[0], up2))
            - scale[7 * M + m] * up
        )
        first_down = (
            commuted(
                plainly(hamiltonian, down),
                with_factor(below_op[0], down2, *factor(scale, 2, m)),
            )
            - scale[8 * M + m] * down
        )
        second = part[turn] + second_of(scale, m, hamiltonian, up_op, down_op, first, first_up, first_down)
        if last:
            plain[turn, 0] = total[turn] + (1.0 / 6.0) * first + (1.0 / 24.0) * second
            pack(plain.at[turn, 0], result.at[turn])
        else:
            kept_first[turn] = first
            plain[turn, 0] = second
            pack(plain.at[turn, 0], raw.at[turn, 0])
            for member in range(MEMBERS):
                result[member, pl.ds(m * PIECE, PIECE), :] = raw[turn, 0, member * PIECE : (member + 1) * PIECE, :]


TOGETHER = 2
PLAIN = pl.BlockSpec((TOGETHER, 2 * N, 128), lambda step, scale: (step, 0, 0))
WHOLE = pl.BlockSpec((TOGETHER, ROWS, 128), lambda step, scale: (step, 0, 0))
SUMS = pltpu.HBM((M, 2 * N, 128), F32)


def all_of(shape):
    return pl.BlockSpec(shape, lambda step, scale: (0,) * len(shape))


def operator_specs(*lists):
    return [
        pl.BlockSpec((1, 2, N, CHUNK), lambda step, scale, at=at * M + turn: (step * TOGETHER + at, 0, 0, 0))
        for turn in range(TOGETHER)
        for at in lists
    ]


def by_matrix(kernel, name, in_specs, out_specs, out_shape, raws, plains):
    return pl.pallas_call(
        kernel,
        grid_spec=pltpu.PrefetchScalarGridSpec(
            num_scalar_prefetch=1,
            grid=(M // TOGETHER,),
            in_specs=in_specs,
            out_specs=out_specs,
            scratch_shapes=[pltpu.VMEM((TOGETHER, raws, ROWS, 128), F32), pltpu.VMEM((TOGETHER, plains, 2 * N, 128), F32)],
        ),
        out_shape=out_shape,
        compiler_params=pltpu.CompilerParams(vmem_limit_bytes=32 * 1024 * 1024),
        name=name,
    )


HAMILTONIAN = pl.BlockSpec((1, 2, N, CHUNK), lambda step, scale: (6 * M, 0, 0, 0))


def kept(*values):
    return [pltpu.with_memory_space_constraint(value, pltpu.HBM) for value in values]


def early(scale, state, near, operators, sums):
    last = len(sums) > 0
    specs = [all_of(state.shape) if last else WHOLE, all_of(near.shape), HAMILTONIAN]
    specs += operator_specs(0, 3, 4, 2) + [PLAIN] * len(sums)
    call = by_matrix(functools.partial(early_kernel, last), "early", specs, [PLAIN] * 2, [SUMS] * 2, 3, 3)
    return call(scale, state, near, *kept(*[operators] * (4 * TOGETHER + 1), *sums))


def late(scale, other, operators, part, total):
    last = total is not None
    specs = [pl.BlockSpec((MEMBERS, TOGETHER * 4 * PIECE, 128), lambda step, scale: (0, step, 0))]
    specs += [HAMILTONIAN] + operator_specs(0, 3, 1, 5) + [PLAIN] * (1 + last)
    if last:
        outs = [WHOLE], [jax.ShapeDtypeStruct((M, ROWS, 128), F32)]
    else:
        blocks = (MEMBERS, M * PIECE, 128)
        outs = [all_of(blocks), PLAIN], [pltpu.HBM(blocks, F32), SUMS]
    call = by_matrix(functools.partial(late_kernel, last), "late", specs, *outs, 4, 4)
    return call(scale, other, *kept(*[operators] * (4 * TOGETHER + 1), part, *[total] * last))


def shards(
    density,
    hamiltonian,
    coupling,
    decay_rate,
    corr_real,
    corr_imag,
    up_member,
    up_slot,
    up_mode,
    down_member,
    down_slot,
    down_mode,
):
    tier, member = lax.axis_index("tier"), lax.axis_index("member")
    fields = jnp.stack([f[:, 0] for f in (up_member, up_slot, up_mode, down_member, down_slot, down_mode)])
    fields = fields.reshape(1, FIELDS).astype(F32)
    links = jnp.pad(fields, ((0, 7), (0, 128 - FIELDS)))
    place = jnp.stack([tier, member]).astype(jnp.int32)
    levels = jnp.stack([tier, tier + 1, tier - 1]).astype(F32)
    ups = jnp.where(levels + 1.0 < TIERS, jnp.sqrt(levels + 1.0), 0.0)
    downs = jnp.sqrt(jnp.maximum(levels, 0.0))
    weight = STEP * jnp.concatenate([ups, downs])

    def swapped(blocks):
        return lax.all_to_all(blocks, "member", split_axis=0, concat_axis=0, tiled=True)

    def link_fields(tier_blocks):
        return tier_blocks[:, M * PIECE, :FIELDS].reshape(-1).astype(jnp.int32)

    def two_steps(own, find, links, state, operators, scale, sums):
        mate = lax.ppermute(own, "tier", [(source, source ^ 1) for source in range(TIERS)])
        above2, below2 = passed_along(own, -2), passed_along(own, 2)
        near = swapped(picked(functools.partial(pick_near_kernel, find), 2, [links], [own]))
        cross = jnp.where(tier % 2 == 0, above2, below2)
        cross = lax.ppermute(cross, "tier", [(source, source ^ 1) for source in range(TIERS)])
        other = swapped(picked(functools.partial(pick_other_kernel, find), 4, [links, place], [mate, cross, above2, below2]))
        part, total = early(scale, state, near, operators, sums)
        return total, late(scale, other, operators, part, total if sums else None)

    state = density.reshape(M, 2, ROWS // 2, 128).transpose(0, 2, 1, 3).reshape(M, ROWS, 128)
    own = swapped(dealt(state, links))
    table = link_fields(own)
    table = jnp.concatenate([table, passed_along(table, -1), passed_along(table, 1)])
    own, table = lax.optimization_barrier((own, table))
    mode, scale, lists = make_nodes(table, place, corr_real, corr_imag, decay_rate, weight)
    operators = make_operators(mode, scale, hamiltonian, coupling)
    start, (blocks, first) = two_steps(own, chased, table, state, operators, scale, ())
    _, (result,) = two_steps(swapped(blocks), listed, lists, blocks, operators, scale, (start, first))
    return result.reshape(M, ROWS // 2, 2, 128).transpose(0, 2, 1, 3).reshape(M, 2, N * N)


def solution(mesh):
    return jax.shard_map(
        shards,
        mesh=mesh,
        in_specs=(P(("tier", "member"), None, None),) + (P(),) * 5 + (P(("tier", "member"), None),) * 6,
        out_specs=P(("tier", "member"), None, None),
        check_vma=False,
    )
```

```python
import functools

import jax
import jax.numpy as jnp
from jax import lax
from jax.experimental import pallas as pl
from jax.experimental.pallas import tpu as pltpu
from jax.sharding import PartitionSpec as P

STEP = 0.08
N = 96
M = 8
ROWS = 144
PIECE = 9
MEMBERS = 16
TIERS = 8
WEIGHT = 9 * M
FIELDS = 6 * M
F32 = jnp.float32
BF16 = jnp.bfloat16
CHUNK = 128


def passed_along(value, steps):
    low, high = max(0, -steps), min(TIERS, TIERS - steps)
    return lax.ppermute(value, "tier", [(source, source + steps) for source in range(low, high)])


def entry(table, level, member, field, slot):
    return table[(level * MEMBERS + member) * FIELDS + field * M + slot]


def nodes_kernel(table, place, corr_real, corr_imag, decay, weight, mode, scale, lists):
    tier, member = place[0], place[1]
    level = tier.astype(F32)

    def node(at, where, rate):
        down_mode = entry(table, *where[:2], 5, where[2])
        mode[at] = entry(table, *where[:2], 2, where[2])
        mode[3 * M + at] = down_mode
        scale[at] = corr_real[down_mode]
        scale[3 * M + at] = corr_imag[down_mode]
        scale[6 * M + at] = rate * decay[down_mode]

    def one(m, carry):
        node(m, (0, member, m), STEP * level)
        node(M + m, (1, entry(table, 0, member, 0, m), entry(table, 0, member, 1, m)), STEP * (level + 1.0))
        node(
            2 * M + m,
            (2, entry(table, 0, member, 3, m), entry(table, 0, member, 4, m)),
            STEP * jnp.maximum(level - 1.0, 0.0),
        )
        return carry

    lax.fori_loop(0, M, one, 0)
    for kind in range(6):
        scale[WEIGHT + kind] = weight[kind]

    def note(member, carry):
        for m in range(M):
            for kind in range(2):
                for far in range(3):
                    who, slot = chased(table, member, m, kind, far)
                    lists[(member * M + m) * 6 + kind * 3 + far] = who * M + slot
        return carry

    lax.fori_loop(0, MEMBERS, note, 0)


def make_nodes(table, place, corr_real, corr_imag, decay, weight):
    smem = pl.BlockSpec(memory_space=pltpu.SMEM)
    return pl.pallas_call(
        nodes_kernel,
        in_specs=[smem] * 6,
        out_specs=[smem] * 3,
        out_shape=[
            jax.ShapeDtypeStruct((6 * M,), jnp.int32),
            jax.ShapeDtypeStruct((WEIGHT + 6,), F32),
            jax.ShapeDtypeStruct((MEMBERS * M * 6,), jnp.int32),
        ],
        name="nodes",
    )(table, place, corr_real, corr_imag, decay, weight)


def split(value):
    high = value.astype(BF16)
    return high, (value - high.astype(F32)).astype(BF16)


def deal_kernel(state, links, out):
    for member in range(MEMBERS):
        for m in range(M):
            out[member, m * PIECE : (m + 1) * PIECE, :] = state[m, member * PIECE : (member + 1) * PIECE, :]
        out[member, M * PIECE :, :] = links[...]


def dealt(state, links):
    return pl.pallas_call(
        deal_kernel,
        out_shape=jax.ShapeDtypeStruct((MEMBERS, M * PIECE + 8, 128), F32),
        compiler_params=pltpu.CompilerParams(vmem_limit_bytes=16 * 1024 * 1024),
        name="deal",
    )(state, links)


def chased(table, member, m, kind, far):
    first = 3 * kind
    who, slot = entry(table, 0, member, first, m), entry(table, 0, member, first + 1, m)
    if far:
        then = first if far == 1 else 3 - first
        who, slot = (entry(table, kind + 1, who, then + field, slot) for field in range(2))
    return who, slot


def listed(lists, member, m, kind, far):
    place = lists[(member * M + m) * 6 + kind * 3 + far]
    return lax.shift_right_logical(place, 3), jnp.bitwise_and(place, M - 1)


def sent_out(held, out, done, member):
    return pltpu.make_async_copy(held.at[member], out.at[member], done.at[member])


def pick_near_kernel(find, links, own, out, held, done):
    def one(member, carry):
        for m in range(M):
            for kind in range(2):
                who, slot = find(links, member, m, kind, 2)
                row = (kind * M + m) * PIECE
                held[member, row : row + PIECE, :] = own[who, pl.ds(slot * PIECE, PIECE), :]
        sent_out(held, out, done, member).start()
        return carry

    lax.fori_loop(0, MEMBERS, one, 0)
    for member in range(MEMBERS):
        sent_out(held, out, done, member).wait()


def pick_other_kernel(find, links, place, mate, cross, above2, below2, out, held, done):
    def one(above, below, member, carry):
        for m in range(M):
            for kind, source, source2 in ((0, above, above2), (1, below, below2)):
                who, slot = find(links, member, m, kind, 0)
                row = (m * 4 + kind) * PIECE
                held[member, row : row + PIECE, :] = source[who, pl.ds(slot * PIECE, PIECE), :]
                who, slot = find(links, member, m, kind, 1)
                row += 2 * PIECE
                held[member, row : row + PIECE, :] = source2[who, pl.ds(slot * PIECE, PIECE), :]
        sent_out(held, out, done, member).start()
        return carry

    lower_core = jnp.bitwise_and(place[0], 1) == 0
    pl.when(lower_core)(lambda: lax.fori_loop(0, MEMBERS, functools.partial(one, mate, cross), None))
    pl.when(jnp.logical_not(lower_core))(lambda: lax.fori_loop(0, MEMBERS, functools.partial(one, cross, mate), None))
    for member in range(MEMBERS):
        sent_out(held, out, done, member).wait()


def picked(kernel, kinds, scalars, blocks):
    shape = (MEMBERS, kinds * M * PIECE, 128)
    return pl.pallas_call(
        kernel,
        in_specs=[pl.BlockSpec(memory_space=pltpu.SMEM)] * len(scalars)
        + [pl.BlockSpec(memory_space=pltpu.VMEM)] * len(blocks),
        out_specs=pl.BlockSpec(memory_space=pl.ANY),
        out_shape=pltpu.HBM(shape, F32),
        scratch_shapes=[pltpu.VMEM(shape, F32), pltpu.SemaphoreType.DMA((MEMBERS,))],
        compiler_params=pltpu.CompilerParams(vmem_limit_bytes=16 * 1024 * 1024),
        name="pick",
    )(*scalars, *blocks)


def unpack(source, target):
    lane = lax.broadcasted_iota(jnp.int32, (24, 128), 1)
    for part in range(2):
        a, b, c = (source[pl.ds(2 * k + part, 24, stride=6), :] for k in range(3))
        target[pl.ds(part * N, 24, stride=4), :] = a
        target[pl.ds(part * N + 1, 24, stride=4), :] = jnp.where(lane < 32, pltpu.roll(a, 32, 1), pltpu.roll(b, 32, 1))
        target[pl.ds(part * N + 2, 24, stride=4), :] = jnp.where(lane < 64, pltpu.roll(b, 64, 1), pltpu.roll(c, 64, 1))
        target[pl.ds(part * N + 3, 24, stride=4), :] = pltpu.roll(c, 96, 1)


def pack(source, target):
    lane = lax.broadcasted_iota(jnp.int32, (24, 128), 1)
    for part in range(2):
        a, b, c, d = (source[pl.ds(part * N + k, 24, stride=4), :] for k in range(4))
        b, c, d = pltpu.roll(b, 96, 1), pltpu.roll(c, 64, 1), pltpu.roll(d, 32, 1)
        target[pl.ds(part, 24, stride=6), :] = jnp.where(lane < 96, a, b)
        target[pl.ds(part + 2, 24, stride=6), :] = jnp.where(lane < 64, b, c)
        target[pl.ds(part + 4, 24, stride=6), :] = jnp.where(lane < 32, c, d)


def halved(value):
    high, low = split(value)
    return (high[:N], high[N:]), (low[:N], low[N:])


def commuted(*terms):
    lefts, tall, wide_high, wide_low, both, highs = [], [], [], [], [], []
    pad = jnp.zeros((CHUNK - N, 2 * CHUNK), BF16)
    for operator, a, b in terms:
        high, low = operator[0], operator[1]
        lefts += [high, low, high]
        both += [jnp.concatenate([high, low], axis=1), pad]
        highs += [high, pad[:, :CHUNK]]
        high, low = (jnp.concatenate(piece, axis=1) for piece in a)
        tall += [high, pad, high, pad, low, pad]
        high, low = (jnp.concatenate(piece, axis=0) for piece in b)
        wide_high.append(high)
        wide_low.append(low)

    def product(left, right):
        return jnp.dot(jnp.concatenate(left, axis=1), jnp.concatenate(right, axis=0), preferred_element_type=F32)

    from_left = product(lefts, tall)
    from_right = product(wide_high, both)
    from_right = from_right[:, :CHUNK] + from_right[:, CHUNK:] + product(wide_low, highs)
    return jnp.concatenate([from_left[:, CHUNK:] - from_right[N:], from_right[:N] - from_left[:, :CHUNK]], axis=0)


def plainly(operator, value):
    pieces = halved(value)
    return operator, pieces, pieces


def with_factor(operator, value, cr, ci):
    dr, di = value[:N], value[N:]
    rr, ri, ir, ii = cr * dr, cr * di, ci * dr, ci * di
    a, b = jnp.concatenate([rr - ii, ir + ri], axis=0), jnp.concatenate([rr + ii, ri - ir], axis=0)
    return operator, halved(a), halved(b)


def assembled(source, row, raw, target):
    for member in range(MEMBERS):
        raw[member * PIECE : (member + 1) * PIECE, :] = source[member, pl.ds(row, PIECE), :]
    unpack(raw, target)


def operators_kernel(mode, scale, hamiltonian, coupling, out, held, done):
    copies = [pltpu.make_async_copy(coupling.at[mode[at]], held.at[at], done.at[at]) for at in range(6 * M)]
    for copy in copies:
        copy.start()

    def keep(at, operator):
        operator = jnp.concatenate([operator, jnp.zeros((N, CHUNK - N), F32)], axis=1)
        out[at, 0], out[at, 1] = split(operator)

    keep(6 * M, STEP * hamiltonian[...])
    for at, copy in enumerate(copies):
        copy.wait()
        keep(at, scale[WEIGHT + at // M] * held[at])


def make_operators(mode, scale, hamiltonian, coupling):
    smem, vmem = pl.BlockSpec(memory_space=pltpu.SMEM), pl.BlockSpec(memory_space=pltpu.VMEM)
    return pl.pallas_call(
        operators_kernel,
        in_specs=[smem, smem, vmem, pl.BlockSpec(memory_space=pl.ANY)],
        out_specs=vmem,
        out_shape=pltpu.HBM((6 * M + 1, 2, N, CHUNK), BF16),
        scratch_shapes=[pltpu.VMEM((6 * M, N, N), F32), pltpu.SemaphoreType.DMA((6 * M,))],
        compiler_params=pltpu.CompilerParams(vmem_limit_bytes=16 * 1024 * 1024),
        name="operators",
    )(mode, scale, hamiltonian, coupling)


def factor(scale, kind, m):
    return scale[kind * M + m], scale[3 * M + kind * M + m]


def early_kernel(last, scale, state, near, core, *refs):
    ops, refs = refs[: 4 * TOGETHER], refs[4 * TOGETHER :]
    part, total, raw, plain = refs[-4:]
    hamiltonian = core[0]
    for turn in range(TOGETHER):
        m = pl.program_id(0) * TOGETHER + turn
        up_op, down_op, above_op, below_op = ops[4 * turn : 4 * turn + 4]
        if last:
            assembled(state, m * PIECE, raw.at[turn, 0], plain.at[turn, 0])
        else:
            raw[turn, 0, 0:ROWS, :] = state[turn]
            unpack(raw.at[turn, 0], plain.at[turn, 0])
        for kind in range(2):
            assembled(near, (kind * M + m) * PIECE, raw.at[turn, 1 + kind], plain.at[turn, 1 + kind])
        own, up_down, down_up = (plain[turn, place, 0 : 2 * N, :] for place in range(3))
        first = commuted(plainly(hamiltonian, own)) - scale[6 * M + m] * own
        first_up = commuted(with_factor(above_op[0], up_down, *factor(scale, 1, m)))
        first_down = commuted(plainly(below_op[0], down_up))
        part[turn] = second_of(scale, m, hamiltonian, up_op, down_op, first, first_up, first_down)
        if last:
            before, before_first = refs[:2]
            total[turn] = before[turn] + before_first[turn] + 0.5 * own + (1.0 / 6.0) * first
        else:
            total[turn] = own + first


def second_of(scale, m, hamiltonian, up_op, down_op, first, first_up, first_down):
    return (
        commuted(
            plainly(hamiltonian, first),
            plainly(up_op[0], first_up),
            with_factor(down_op[0], first_down, *factor(scale, 0, m)),
        )
        - scale[6 * M + m] * first
    )


def late_kernel(last, scale, other, core, *refs):
    ops, part, refs = refs[: 4 * TOGETHER], refs[4 * TOGETHER], refs[4 * TOGETHER + 1 :]
    if last:
        total, result, raw, plain = refs
    else:
        result, kept_first, raw, plain = refs
    hamiltonian = core[0]
    for turn in range(TOGETHER):
        m = pl.program_id(0) * TOGETHER + turn
        up_op, down_op, above_op, below_op = ops[4 * turn : 4 * turn + 4]
        for kind in range(4):
            assembled(other, (turn * 4 + kind) * PIECE, raw.at[turn, kind], plain.at[turn, kind])
        up, down, up2, down2 = (plain[turn, kind, 0 : 2 * N, :] for kind in range(4))
        up_pieces = halved(up)
        first = commuted(
            (up_op[0], up_pieces, up_pieces),
            with_factor(down_op[0], down, *factor(scale, 0, m)),
        )
        first_up = (
            commuted((hamiltonian, up_pieces, up_pieces), plainly(above_op[0], up2))
            - scale[7 * M + m] * up
        )
        first_down = (
            commuted(
                plainly(hamiltonian, down),
                with_factor(below_op[0], down2, *factor(scale, 2, m)),
            )
            - scale[8 * M + m] * down
        )
        second = part[turn] + second_of(scale, m, hamiltonian, up_op, down_op, first, first_up, first_down)
        if last:
            plain[turn, 0, 0 : 2 * N, :] = total[turn] + (1.0 / 6.0) * first + (1.0 / 24.0) * second
            pack(plain.at[turn, 0], raw.at[turn, 0])
            result[turn] = raw[turn, 0, 0:ROWS, :]
        else:
            kept_first[turn] = first
            plain[turn, 0, 0 : 2 * N, :] = second
            pack(plain.at[turn, 0], raw.at[turn, 0])
            for member in range(MEMBERS):
                result[member, pl.ds(m * PIECE, PIECE), :] = raw[turn, 0, member * PIECE : (member + 1) * PIECE, :]


TOGETHER = 2
PLAIN = pl.BlockSpec((TOGETHER, 2 * N, 128), lambda step, scale: (step, 0, 0))
WHOLE = pl.BlockSpec((TOGETHER, ROWS, 128), lambda step, scale: (step, 0, 0))
SUMS = pltpu.HBM((M, 2 * N, 128), F32)


def all_of(shape):
    return pl.BlockSpec(shape, lambda step, scale: (0,) * len(shape))


def operator_specs(*lists):
    return [
        pl.BlockSpec((1, 2, N, CHUNK), lambda step, scale, at=at * M + turn: (step * TOGETHER + at, 0, 0, 0))
        for turn in range(TOGETHER)
        for at in lists
    ]


def by_matrix(kernel, name, in_specs, out_specs, out_shape, raws, plains):
    return pl.pallas_call(
        kernel,
        grid_spec=pltpu.PrefetchScalarGridSpec(
            num_scalar_prefetch=1,
            grid=(M // TOGETHER,),
            in_specs=in_specs,
            out_specs=out_specs,
            scratch_shapes=[pltpu.VMEM((TOGETHER, raws, ROWS + 8, 128), F32), pltpu.VMEM((TOGETHER, plains, 2 * N + 8, 128), F32)],
        ),
        out_shape=out_shape,
        compiler_params=pltpu.CompilerParams(vmem_limit_bytes=32 * 1024 * 1024),
        name=name,
    )


HAMILTONIAN = pl.BlockSpec((1, 2, N, CHUNK), lambda step, scale: (6 * M, 0, 0, 0))


def kept(*values):
    return [pltpu.with_memory_space_constraint(value, pltpu.HBM) for value in values]


def early(scale, state, near, operators, sums):
    last = len(sums) > 0
    specs = [all_of(state.shape) if last else WHOLE, all_of(near.shape), HAMILTONIAN]
    specs += operator_specs(0, 3, 4, 2) + [PLAIN] * len(sums)
    call = by_matrix(functools.partial(early_kernel, last), "early", specs, [PLAIN] * 2, [SUMS] * 2, 3, 3)
    return call(scale, state, near, *kept(*[operators] * (4 * TOGETHER + 1), *sums))


def late(scale, other, operators, part, total):
    last = total is not None
    specs = [pl.BlockSpec((MEMBERS, TOGETHER * 4 * PIECE, 128), lambda step, scale: (0, step, 0))]
    specs += [HAMILTONIAN] + operator_specs(0, 3, 1, 5) + [PLAIN] * (1 + last)
    if last:
        outs = [WHOLE], [jax.ShapeDtypeStruct((M, ROWS, 128), F32)]
    else:
        blocks = (MEMBERS, M * PIECE, 128)
        outs = [all_of(blocks), PLAIN], [pltpu.HBM(blocks, F32), SUMS]
    call = by_matrix(functools.partial(late_kernel, last), "late", specs, *outs, 4, 4)
    return call(scale, other, *kept(*[operators] * (4 * TOGETHER + 1), part, *[total] * last))


def shards(
    density,
    hamiltonian,
    coupling,
    decay_rate,
    corr_real,
    corr_imag,
    up_member,
    up_slot,
    up_mode,
    down_member,
    down_slot,
    down_mode,
):
    tier, member = lax.axis_index("tier"), lax.axis_index("member")
    fields = jnp.stack([f[:, 0] for f in (up_member, up_slot, up_mode, down_member, down_slot, down_mode)])
    fields = fields.reshape(1, FIELDS).astype(F32)
    links = jnp.pad(fields, ((0, 7), (0, 128 - FIELDS)))
    place = jnp.stack([tier, member]).astype(jnp.int32)
    levels = jnp.stack([tier, tier + 1, tier - 1]).astype(F32)
    ups = jnp.where(levels + 1.0 < TIERS, jnp.sqrt(levels + 1.0), 0.0)
    downs = jnp.sqrt(jnp.maximum(levels, 0.0))
    weight = STEP * jnp.concatenate([ups, downs])

    def swapped(blocks):
        return lax.all_to_all(blocks, "member", split_axis=0, concat_axis=0, tiled=True)

    def link_fields(tier_blocks):
        return tier_blocks[:, M * PIECE, :FIELDS].reshape(-1).astype(jnp.int32)

    def two_steps(own, find, links, state, operators, scale, sums):
        mate = lax.ppermute(own, "tier", [(source, source ^ 1) for source in range(TIERS)])
        above2, below2 = passed_along(own, -2), passed_along(own, 2)
        near = swapped(picked(functools.partial(pick_near_kernel, find), 2, [links], [own]))
        cross = jnp.where(tier % 2 == 0, above2, below2)
        cross = lax.ppermute(cross, "tier", [(source, source ^ 1) for source in range(TIERS)])
        other = swapped(picked(functools.partial(pick_other_kernel, find), 4, [links, place], [mate, cross, above2, below2]))
        part, total = early(scale, state, near, operators, sums)
        return total, late(scale, other, operators, part, total if sums else None)

    state = density.reshape(M, 2, ROWS // 2, 128).transpose(0, 2, 1, 3).reshape(M, ROWS, 128)
    own = swapped(dealt(state, links))
    table = link_fields(own)
    table = jnp.concatenate([table, passed_along(table, -1), passed_along(table, 1)])
    own, table = lax.optimization_barrier((own, table))
    mode, scale, lists = make_nodes(table, place, corr_real, corr_imag, decay_rate, weight)
    operators = make_operators(mode, scale, hamiltonian, coupling)
    start, (blocks, first) = two_steps(own, chased, table, state, operators, scale, ())
    _, (result,) = two_steps(swapped(blocks), listed, lists, blocks, operators, scale, (start, first))
    return result.reshape(M, ROWS // 2, 2, 128).transpose(0, 2, 1, 3).reshape(M, 2, N * N)


def solution(mesh):
    return jax.shard_map(
        shards,
        mesh=mesh,
        in_specs=(P(("tier", "member"), None, None),) + (P(),) * 5 + (P(("tier", "member"), None),) * 6,
        out_specs=P(("tier", "member"), None, None),
        check_vma=False,
    )
```

```python
import functools

import jax
import jax.numpy as jnp
from jax import lax
from jax.experimental import pallas as pl
from jax.experimental.pallas import tpu as pltpu
from jax.sharding import PartitionSpec as P

STEP = 0.08
N = 96
M = 8
ROWS = 144
PIECE = 9
MEMBERS = 16
TIERS = 8
WEIGHT = 9 * M
FIELDS = 6 * M
F32 = jnp.float32
BF16 = jnp.bfloat16
CHUNK = 128


def passed_along(value, steps):
    low, high = max(0, -steps), min(TIERS, TIERS - steps)
    return lax.ppermute(value, "tier", [(source, source + steps) for source in range(low, high)])


def entry(table, level, member, field, slot):
    return table[(level * MEMBERS + member) * FIELDS + field * M + slot]


def nodes_kernel(table, place, corr_real, corr_imag, decay, weight, mode, scale, lists):
    tier, member = place[0], place[1]
    level = tier.astype(F32)

    def node(at, where, rate):
        down_mode = entry(table, *where[:2], 5, where[2])
        mode[at] = entry(table, *where[:2], 2, where[2])
        mode[3 * M + at] = down_mode
        scale[at] = corr_real[down_mode]
        scale[3 * M + at] = corr_imag[down_mode]
        scale[6 * M + at] = rate * decay[down_mode]

    def one(m, carry):
        node(m, (0, member, m), STEP * level)
        node(M + m, (1, entry(table, 0, member, 0, m), entry(table, 0, member, 1, m)), STEP * (level + 1.0))
        node(
            2 * M + m,
            (2, entry(table, 0, member, 3, m), entry(table, 0, member, 4, m)),
            STEP * jnp.maximum(level - 1.0, 0.0),
        )
        return carry

    lax.fori_loop(0, M, one, 0)
    for kind in range(6):
        scale[WEIGHT + kind] = weight[kind]

    def note(member, carry):
        for m in range(M):
            for kind in range(2):
                for far in range(3):
                    who, slot = chased(table, member, m, kind, far)
                    lists[(member * M + m) * 6 + kind * 3 + far] = who * M + slot
        return carry

    lax.fori_loop(0, MEMBERS, note, 0)


def make_nodes(table, place, corr_real, corr_imag, decay, weight):
    smem = pl.BlockSpec(memory_space=pltpu.SMEM)
    return pl.pallas_call(
        nodes_kernel,
        in_specs=[smem] * 6,
        out_specs=[smem] * 3,
        out_shape=[
            jax.ShapeDtypeStruct((6 * M,), jnp.int32),
            jax.ShapeDtypeStruct((WEIGHT + 6,), F32),
            jax.ShapeDtypeStruct((MEMBERS * M * 6,), jnp.int32),
        ],
        name="nodes",
    )(table, place, corr_real, corr_imag, decay, weight)


def split(value):
    high = value.astype(BF16)
    return high, (value - high.astype(F32)).astype(BF16)


def deal_kernel(state, links, out):
    for member in range(MEMBERS):
        for m in range(M):
            out[member, m * PIECE : (m + 1) * PIECE, :] = state[m, member * PIECE : (member + 1) * PIECE, :]
        out[member, M * PIECE :, :] = links[...]


def dealt(state, links):
    return pl.pallas_call(
        deal_kernel,
        out_shape=jax.ShapeDtypeStruct((MEMBERS, M * PIECE + 8, 128), F32),
        compiler_params=pltpu.CompilerParams(vmem_limit_bytes=16 * 1024 * 1024),
        name="deal",
    )(state, links)


def chased(table, member, m, kind, far):
    first = 3 * kind
    who, slot = entry(table, 0, member, first, m), entry(table, 0, member, first + 1, m)
    if far:
        then = first if far == 1 else 3 - first
        who, slot = (entry(table, kind + 1, who, then + field, slot) for field in range(2))
    return who, slot


def listed(lists, member, m, kind, far):
    place = lists[(member * M + m) * 6 + kind * 3 + far]
    return lax.shift_right_logical(place, 3), jnp.bitwise_and(place, M - 1)


def sent_out(held, out, done, member):
    return pltpu.make_async_copy(held.at[member], out.at[member], done.at[member])


def pick_near_kernel(find, links, own, out, held, done):
    def one(member, carry):
        for m in range(M):
            for kind in range(2):
                who, slot = find(links, member, m, kind, 2)
                row = (kind * M + m) * PIECE
                held[member, row : row + PIECE, :] = own[who, pl.ds(slot * PIECE, PIECE), :]
        sent_out(held, out, done, member).start()
        return carry

    lax.fori_loop(0, MEMBERS, one, 0)
    for member in range(MEMBERS):
        sent_out(held, out, done, member).wait()


def pick_other_kernel(find, links, place, mate, cross, above2, below2, out, held, done):
    def one(above, below, member, carry):
        for m in range(M):
            for kind, source, source2 in ((0, above, above2), (1, below, below2)):
                who, slot = find(links, member, m, kind, 0)
                row = (m * 4 + kind) * PIECE
                held[member, row : row + PIECE, :] = source[who, pl.ds(slot * PIECE, PIECE), :]
                who, slot = find(links, member, m, kind, 1)
                row += 2 * PIECE
                held[member, row : row + PIECE, :] = source2[who, pl.ds(slot * PIECE, PIECE), :]
        sent_out(held, out, done, member).start()
        return carry

    lower_core = jnp.bitwise_and(place[0], 1) == 0
    pl.when(lower_core)(lambda: lax.fori_loop(0, MEMBERS, functools.partial(one, mate, cross), None))
    pl.when(jnp.logical_not(lower_core))(lambda: lax.fori_loop(0, MEMBERS, functools.partial(one, cross, mate), None))
    for member in range(MEMBERS):
        sent_out(held, out, done, member).wait()


def picked(kernel, kinds, scalars, blocks):
    shape = (MEMBERS, kinds * M * PIECE, 128)
    return pl.pallas_call(
        kernel,
        in_specs=[pl.BlockSpec(memory_space=pltpu.SMEM)] * len(scalars)
        + [pl.BlockSpec(memory_space=pltpu.VMEM)] * len(blocks),
        out_specs=pl.BlockSpec(memory_space=pl.ANY),
        out_shape=pltpu.HBM(shape, F32),
        scratch_shapes=[pltpu.VMEM(shape, F32), pltpu.SemaphoreType.DMA((MEMBERS,))],
        compiler_params=pltpu.CompilerParams(vmem_limit_bytes=16 * 1024 * 1024),
        name="pick",
    )(*scalars, *blocks)


def unpack(source, target):
    lane = lax.broadcasted_iota(jnp.int32, (24, 128), 1)
    for part in range(2):
        a, b, c = (source[pl.ds(2 * k + part, 24, stride=6), :] for k in range(3))
        target[pl.ds(part * N, 24, stride=4), :] = a
        target[pl.ds(part * N + 1, 24, stride=4), :] = jnp.where(lane < 32, pltpu.roll(a, 32, 1), pltpu.roll(b, 32, 1))
        target[pl.ds(part * N + 2, 24, stride=4), :] = jnp.where(lane < 64, pltpu.roll(b, 64, 1), pltpu.roll(c, 64, 1))
        target[pl.ds(part * N + 3, 24, stride=4), :] = pltpu.roll(c, 96, 1)


def pack(source, target):
    lane = lax.broadcasted_iota(jnp.int32, (24, 128), 1)
    for part in range(2):
        a, b, c, d = (source[pl.ds(part * N + k, 24, stride=4), :] for k in range(4))
        b, c, d = pltpu.roll(b, 96, 1), pltpu.roll(c, 64, 1), pltpu.roll(d, 32, 1)
        target[pl.ds(part, 24, stride=6), :] = jnp.where(lane < 96, a, b)
        target[pl.ds(part + 2, 24, stride=6), :] = jnp.where(lane < 64, b, c)
        target[pl.ds(part + 4, 24, stride=6), :] = jnp.where(lane < 32, c, d)


def halved(value):
    high, low = split(value)
    return (high[:N], high[N:]), (low[:N], low[N:])


def commuted(*terms):
    lefts, tall, wide_high, wide_low, both, highs = [], [], [], [], [], []
    pad = jnp.zeros((CHUNK - N, 2 * CHUNK), BF16)
    for operator, a, b in terms:
        high, low = operator[0], operator[1]
        lefts += [high, low, high]
        both += [jnp.concatenate([high, low], axis=1), pad]
        highs += [high, pad[:, :CHUNK]]
        high, low = (jnp.concatenate(piece, axis=1) for piece in a)
        tall += [high, pad, high, pad, low, pad]
        high, low = (jnp.concatenate(piece, axis=0) for piece in b)
        wide_high.append(high)
        wide_low.append(low)

    def product(left, right):
        return jnp.dot(jnp.concatenate(left, axis=1), jnp.concatenate(right, axis=0), preferred_element_type=F32)

    from_left = product(lefts, tall)
    from_right = product(wide_high, both)
    from_right = from_right[:, :CHUNK] + from_right[:, CHUNK:] + product(wide_low, highs)
    return jnp.concatenate([from_left[:, CHUNK:] - from_right[N:], from_right[:N] - from_left[:, :CHUNK]], axis=0)


def plainly(operator, value):
    pieces = halved(value)
    return operator, pieces, pieces


def with_factor(operator, value, cr, ci):
    dr, di = value[:N], value[N:]
    rr, ri, ir, ii = cr * dr, cr * di, ci * dr, ci * di
    a, b = jnp.concatenate([rr - ii, ir + ri], axis=0), jnp.concatenate([rr + ii, ri - ir], axis=0)
    return operator, halved(a), halved(b)


def assembled(source, row, raw, target):
    for member in range(MEMBERS):
        raw[member * PIECE : (member + 1) * PIECE, :] = source[member, pl.ds(row, PIECE), :]
    unpack(raw, target)


def operators_kernel(mode, scale, hamiltonian, coupling, out, held, done):
    copies = [pltpu.make_async_copy(coupling.at[mode[at]], held.at[at], done.at[at]) for at in range(6 * M)]
    for copy in copies:
        copy.start()

    def keep(at, operator):
        operator = jnp.concatenate([operator, jnp.zeros((N, CHUNK - N), F32)], axis=1)
        out[at, 0], out[at, 1] = split(operator)

    keep(6 * M, STEP * hamiltonian[...])
    for at, copy in enumerate(copies):
        copy.wait()
        keep(at, scale[WEIGHT + at // M] * held[at])


def make_operators(mode, scale, hamiltonian, coupling):
    smem, vmem = pl.BlockSpec(memory_space=pltpu.SMEM), pl.BlockSpec(memory_space=pltpu.VMEM)
    return pl.pallas_call(
        operators_kernel,
        in_specs=[smem, smem, vmem, pl.BlockSpec(memory_space=pl.ANY)],
        out_specs=vmem,
        out_shape=pltpu.HBM((6 * M + 1, 2, N, CHUNK), BF16),
        scratch_shapes=[pltpu.VMEM((6 * M, N, N), F32), pltpu.SemaphoreType.DMA((6 * M,))],
        compiler_params=pltpu.CompilerParams(vmem_limit_bytes=16 * 1024 * 1024),
        name="operators",
    )(mode, scale, hamiltonian, coupling)


def factor(scale, kind, m):
    return scale[kind * M + m], scale[3 * M + kind * M + m]


def early_kernel(last, scale, state, near, core, *refs):
    ops, refs = refs[: 4 * TOGETHER], refs[4 * TOGETHER :]
    part, total, raw, plain = refs[-4:]
    hamiltonian = core[0]
    for turn in range(TOGETHER):
        m = pl.program_id(0) * TOGETHER + turn
        up_op, down_op, above_op, below_op = ops[4 * turn : 4 * turn + 4]
        if last:
            assembled(state, m * PIECE, raw.at[turn, 0], plain.at[turn, 0])
        else:
            raw[turn, 0, 0:ROWS, :] = state[turn]
            unpack(raw.at[turn, 0], plain.at[turn, 0])
        for kind in range(2):
            assembled(near, (kind * M + m) * PIECE, raw.at[turn, 1 + kind], plain.at[turn, 1 + kind])
        own, up_down, down_up = (plain[turn, place, 0 : 2 * N, :] for place in range(3))
        first = commuted(plainly(hamiltonian, own)) - scale[6 * M + m] * own
        first_up = commuted(with_factor(above_op[0], up_down, *factor(scale, 1, m)))
        first_down = commuted(plainly(below_op[0], down_up))
        part[turn] = second_of(scale, m, hamiltonian, up_op, down_op, first, first_up, first_down)
        if last:
            before, before_first = refs[:2]
            total[turn] = before[turn] + before_first[turn] + 0.5 * own + (1.0 / 6.0) * first
        else:
            total[turn] = own + first


def second_of(scale, m, hamiltonian, up_op, down_op, first, first_up, first_down):
    return (
        commuted(
            plainly(hamiltonian, first),
            plainly(up_op[0], first_up),
            with_factor(down_op[0], first_down, *factor(scale, 0, m)),
        )
        - scale[6 * M + m] * first
    )


def late_kernel(last, scale, other, core, *refs):
    ops, part, refs = refs[: 4 * TOGETHER], refs[4 * TOGETHER], refs[4 * TOGETHER + 1 :]
    if last:
        total, result, raw, plain = refs
    else:
        result, kept_first, raw, plain = refs
    hamiltonian = core[0]
    for turn in range(TOGETHER):
        m = pl.program_id(0) * TOGETHER + turn
        up_op, down_op, above_op, below_op = ops[4 * turn : 4 * turn + 4]
        for kind in range(4):
            assembled(other, (m * 4 + kind) * PIECE, raw.at[turn, kind], plain.at[turn, kind])
        up, down, up2, down2 = (plain[turn, kind, 0 : 2 * N, :] for kind in range(4))
        up_pieces = halved(up)
        first = commuted(
            (up_op[0], up_pieces, up_pieces),
            with_factor(down_op[0], down, *factor(scale, 0, m)),
        )
        first_up = (
            commuted((hamiltonian, up_pieces, up_pieces), plainly(above_op[0], up2))
            - scale[7 * M + m] * up
        )
        first_down = (
            commuted(
                plainly(hamiltonian, down),
                with_factor(below_op[0], down2, *factor(scale, 2, m)),
            )
            - scale[8 * M + m] * down
        )
        second = part[turn] + second_of(scale, m, hamiltonian, up_op, down_op, first, first_up, first_down)
        if last:
            plain[turn, 0, 0 : 2 * N, :] = total[turn] + (1.0 / 6.0) * first + (1.0 / 24.0) * second
            pack(plain.at[turn, 0], raw.at[turn, 0])
            result[turn] = raw[turn, 0, 0:ROWS, :]
        else:
            kept_first[turn] = first
            plain[turn, 0, 0 : 2 * N, :] = second
            pack(plain.at[turn, 0], raw.at[turn, 0])
            for member in range(MEMBERS):
                result[member, pl.ds(m * PIECE, PIECE), :] = raw[turn, 0, member * PIECE : (member + 1) * PIECE, :]


TOGETHER = 4
PLAIN = pl.BlockSpec((TOGETHER, 2 * N, 128), lambda step, scale: (step, 0, 0))
WHOLE = pl.BlockSpec((TOGETHER, ROWS, 128), lambda step, scale: (step, 0, 0))
SUMS = pltpu.HBM((M, 2 * N, 128), F32)


def all_of(shape):
    return pl.BlockSpec(shape, lambda step, scale: (0,) * len(shape))


def operator_specs(*lists):
    return [
        pl.BlockSpec((1, 2, N, CHUNK), lambda step, scale, at=at * M + turn: (step * TOGETHER + at, 0, 0, 0))
        for turn in range(TOGETHER)
        for at in lists
    ]


def by_matrix(kernel, name, in_specs, out_specs, out_shape, raws, plains):
    return pl.pallas_call(
        kernel,
        grid_spec=pltpu.PrefetchScalarGridSpec(
            num_scalar_prefetch=1,
            grid=(M // TOGETHER,),
            in_specs=in_specs,
            out_specs=out_specs,
            scratch_shapes=[pltpu.VMEM((TOGETHER, raws, ROWS + 8, 128), F32), pltpu.VMEM((TOGETHER, plains, 2 * N + 8, 128), F32)],
        ),
        out_shape=out_shape,
        compiler_params=pltpu.CompilerParams(vmem_limit_bytes=32 * 1024 * 1024),
        name=name,
    )


HAMILTONIAN = pl.BlockSpec((1, 2, N, CHUNK), lambda step, scale: (6 * M, 0, 0, 0))


def kept(*values):
    return [pltpu.with_memory_space_constraint(value, pltpu.HBM) for value in values]


def early(scale, state, near, operators, sums):
    last = len(sums) > 0
    specs = [all_of(state.shape) if last else WHOLE, all_of(near.shape), HAMILTONIAN]
    specs += operator_specs(0, 3, 4, 2) + [PLAIN] * len(sums)
    call = by_matrix(functools.partial(early_kernel, last), "early", specs, [PLAIN] * 2, [SUMS] * 2, 3, 3)
    return call(scale, state, near, *kept(*[operators] * (4 * TOGETHER + 1), *sums))


def late(scale, other, operators, part, total):
    last = total is not None
    specs = [pl.BlockSpec(memory_space=pltpu.VMEM)]
    specs += [HAMILTONIAN] + operator_specs(0, 3, 1, 5) + [PLAIN] * (1 + last)
    if last:
        outs = [WHOLE], [jax.ShapeDtypeStruct((M, ROWS, 128), F32)]
    else:
        blocks = (MEMBERS, M * PIECE, 128)
        outs = [all_of(blocks), PLAIN], [pltpu.HBM(blocks, F32), SUMS]
    call = by_matrix(functools.partial(late_kernel, last), "late", specs, *outs, 4, 4)
    return call(scale, other, *kept(*[operators] * (4 * TOGETHER + 1), part, *[total] * last))


def shards(
    density,
    hamiltonian,
    coupling,
    decay_rate,
    corr_real,
    corr_imag,
    up_member,
    up_slot,
    up_mode,
    down_member,
    down_slot,
    down_mode,
):
    tier, member = lax.axis_index("tier"), lax.axis_index("member")
    fields = jnp.stack([f[:, 0] for f in (up_member, up_slot, up_mode, down_member, down_slot, down_mode)])
    fields = fields.reshape(1, FIELDS).astype(F32)
    links = jnp.pad(fields, ((0, 7), (0, 128 - FIELDS)))
    place = jnp.stack([tier, member]).astype(jnp.int32)
    levels = jnp.stack([tier, tier + 1, tier - 1]).astype(F32)
    ups = jnp.where(levels + 1.0 < TIERS, jnp.sqrt(levels + 1.0), 0.0)
    downs = jnp.sqrt(jnp.maximum(levels, 0.0))
    weight = STEP * jnp.concatenate([ups, downs])

    def swapped(blocks):
        return lax.all_to_all(blocks, "member", split_axis=0, concat_axis=0, tiled=True)

    def link_fields(tier_blocks):
        return tier_blocks[:, M * PIECE, :FIELDS].reshape(-1).astype(jnp.int32)

    def two_steps(own, find, links, state, operators, scale, sums):
        mate = lax.ppermute(own, "tier", [(source, source ^ 1) for source in range(TIERS)])
        above2, below2 = passed_along(own, -2), passed_along(own, 2)
        near = swapped(picked(functools.partial(pick_near_kernel, find), 2, [links], [own]))
        cross = jnp.where(tier % 2 == 0, above2, below2)
        cross = lax.ppermute(cross, "tier", [(source, source ^ 1) for source in range(TIERS)])
        other = swapped(picked(functools.partial(pick_other_kernel, find), 4, [links, place], [mate, cross, above2, below2]))
        part, total = early(scale, state, near, operators, sums)
        return total, late(scale, other, operators, part, total if sums else None)

    state = density.reshape(M, 2, ROWS // 2, 128).transpose(0, 2, 1, 3).reshape(M, ROWS, 128)
    own = swapped(dealt(state, links))
    table = link_fields(own)
    table = jnp.concatenate([table, passed_along(table, -1), passed_along(table, 1)])
    own, table = lax.optimization_barrier((own, table))
    mode, scale, lists = make_nodes(table, place, corr_real, corr_imag, decay_rate, weight)
    operators = make_operators(mode, scale, hamiltonian, coupling)
    start, (blocks, first) = two_steps(own, chased, table, state, operators, scale, ())
    _, (result,) = two_steps(swapped(blocks), listed, lists, blocks, operators, scale, (start, first))
    return result.reshape(M, ROWS // 2, 2, 128).transpose(0, 2, 1, 3).reshape(M, 2, N * N)


def solution(mesh):
    return jax.shard_map(
        shards,
        mesh=mesh,
        in_specs=(P(("tier", "member"), None, None),) + (P(),) * 5 + (P(("tier", "member"), None),) * 6,
        out_specs=P(("tier", "member"), None, None),
        check_vma=False,
    )
```
